128 devices in a mesh: dp: 16 (over x, z_hi, core), tensor: 8 (over z_lo, y).
Axes of the slice: x: 4, y: 4, z: 4 (z_hi: 2, z_lo: 2; z = z_hi * 2 + z_lo), core: 2. Of those that a mesh axis runs over, the one named last changes fastest.
Arguments:
- hidden_in: bfloat16 [16384, 4096], P(('dp', 'tensor')), may hold values from -6 to 6
- block_output_gradient: bfloat16 [16384, 4096], P(('dp', 'tensor')), may hold values from -6 to 6
- rms_norm_gain: float32 [4096], replicated, may hold values from 0.25 to 1.75
- routes: int32 [16384, 1], P(('dp', 'tensor')), may hold values from 0 to 31; in each aligned block of 128 rows (0 to 127, 128 to 255, ...) at most 6 rows name the same one
- route_weights: bfloat16 [16384, 1], P(('dp', 'tensor')), may hold values from 0.099609375 to 1
- w_gate: bfloat16 [32, 1536, 4096], P('dp', 'tensor'), may hold values from -0.09375 to 0.09375
- w_up: bfloat16 [32, 1536, 4096], P('dp', 'tensor'), may hold values from -0.09375 to 0.09375
- w_down: bfloat16 [32, 1536, 4096], P('dp', 'tensor'), may hold values from -0.15625 to 0.15625
Outputs:
- block_input_gradient: bfloat16 [16384, 4096], P(('dp', 'tensor'))
- norm_gain_gradient: float32 [4096], replicated
- grad_routes: float32 [16384, 1], P(('dp', 'tensor'))
- grad_gate: bfloat16 [32, 1536, 4096], P('dp', 'tensor')
- grad_up: bfloat16 [32, 1536, 4096], P('dp', 'tensor')
- grad_down: bfloat16 [32, 1536, 4096], P('dp', 'tensor')
The draws below stay inside these ranges and needn't reach their ends.
Inputs may be any that keep to these rules, and one draw needn't show every extreme that they name: Each row names one expert. In each aligned block of 128 rows (the rows of one device) no expert is named by more than 6 routes, a bound that some block reaches.
All inputs are finite; a program needn't handle non-finite values.
Results may differ from the reference program's by a relative error of at most 0.0075.
Values may be sent and summed in bfloat16 or wider, within the bound.
No kernel may reach another device: no remote copies, remote signals or barrier semaphores. Data moves between devices by JAX's collectives and lax.ppermute only.
A program may use at most 192 MiB of HBM per device.

```python
import math
import jax
import jax.numpy as jnp
import numpy as np
from jax import lax

D = 4096
FF = 1536
ROUTES = 1
TOK_DEV = 128
EXPERTS = 32
TOKENS = 16384
CAP = 6
N_DP = 16
N_TENSOR = 8


def shard_levels(key, extent, split, low, top_value):
    factor_of = 1.0
    for position, blocks in split:
        draws = jax.random.uniform(jax.random.fold_in(jax.random.fold_in(key, 6), position), (blocks,), jnp.float32, low / len(split), top_value / len(split))
        factor_of = factor_of * jnp.repeat(jnp.exp(draws), extent[position] // blocks).reshape((-1,) + (1,) * (len(extent) - 1 - position))
    return factor_of


def deal_out(own_key, own, number, rows, count, top, limit, lean):
    ranking = jax.random.permutation(own_key, count)
    heavy_load, usual = portions_of(count, rows * top, limit, lean, True), portions_of(count, rows * top, limit, lean, False)
    places = jnp.arange(count)

    def named(sizes, rotation):
        used = int((sizes > 0).sum())
        fixed = max(1, used // 4)
        passed = fixed + (places - fixed + rotation * (used - fixed)) % max(1, count - fixed)
        return jnp.zeros((count,), jnp.int32).at[ranking[jnp.where(places < fixed, places, passed)]].set(jnp.asarray(sizes, jnp.int32))

    sizes = jnp.where(number % 4 == 0, named(heavy_load, number // 4), named(usual, number - number // 4 - 1))
    mixed = jax.random.permutation(jax.random.fold_in(own, 3), count)
    donor, taker = mixed[0:count // 2 * 2:2], mixed[1:count // 2 * 2:2]
    room = jnp.minimum(sizes[donor] - 1, limit - sizes[taker]) // 2
    room = jnp.where((donor == ranking[0]) | (taker == ranking[0]) | (sizes[taker] == 0), 0, jnp.maximum(room, 0))
    passed = jax.random.randint(jax.random.fold_in(own, 4), (count // 2,), 0, 1 << 20) % (room + 1)
    sizes = sizes.at[donor].add(-passed).at[taker].add(passed)
    items = jnp.searchsorted(jnp.cumsum(sizes), jnp.arange(rows * top), side="right").astype(jnp.int32)
    table = items.reshape(top, rows).T
    table = table[jax.random.permutation(jax.random.fold_in(own, 1), rows)]
    rotation = jax.random.randint(jax.random.fold_in(own, 2), (rows, 1), 0, top)
    return jnp.take_along_axis(table, (jnp.arange(top)[None, :] + rotation) % top, axis=1)


def portions_of(count, total, reach, lean, full):
    loads = [(1 << 20) // math.isqrt(standing ** lean) + 1 for standing in range(1, count + 1)]
    largest = reach if full else min(reach, max(-(-total // count), total * loads[0] // sum(loads)))
    least = 1 if total - largest >= count - 1 else 0
    holding, surplus = [largest] + [least] * (count - 1), total - largest - least * (count - 1)
    while surplus > 0:
        free = [i for i in range(1, count) if holding[i] < largest] or [i for i in range(1, count) if holding[i] < reach]
        whole, remaining = sum([loads[i] for i in free]), surplus
        for i in free:
            addition = min(reach - holding[i], max(1, remaining * loads[i] // whole), surplus)
            holding[i] = holding[i] + addition
            surplus = surplus - addition
    return np.array(holding)


def gaussian(rng, shape, scale, reach, shards=(), held_as=jnp.bfloat16):
    result = jax.random.normal(rng, shape, jnp.float32) * scale
    if len(shards) > 0:
        result = shard_levels(rng, shape, shards, -0.22, 0.18) * result
    return jnp.clip(result, min=-reach, max=reach).astype(held_as)


def setup_inputs(seed: int = 0) -> dict:
    key_of = jax.random.split(jax.random.key(seed), 9)
    hidden_in = gaussian(key_of[0], (TOKENS, D), 1.0, 6.0, ((0, 128),))
    block_output_gradient = gaussian(key_of[1], (TOKENS, D), 1.0, 6.0, ((0, 128),))
    rms_norm_gain = jnp.clip(1.0 + 0.15 * jax.random.normal(key_of[2], (D,), jnp.float32), 0.25, 1.75)
    routes_keys = jax.random.split(jax.random.fold_in(key_of[3], 1), TOKENS // TOK_DEV)
    routes_turns = jax.random.permutation(jax.random.fold_in(key_of[3], 3), TOKENS // TOK_DEV)
    routes = jax.vmap(lambda own, number: deal_out(jax.random.fold_in(key_of[3], 2), own, number, TOK_DEV, EXPERTS, ROUTES, CAP, 2))(routes_keys, routes_turns).reshape((TOKENS, ROUTES))
    route_weights = jnp.clip(jnp.exp(math.log(1.0) - 2.306499 * jax.random.uniform(key_of[4], (TOKENS, ROUTES), jnp.float32) ** shard_levels(key_of[4], (TOKENS, ROUTES), ((0, 128),), -0.2, 0.2)), 0.099609375, 1.0).astype(jnp.bfloat16)
    w_gate = gaussian(key_of[5], (EXPERTS, FF, D), D ** -0.5, 0.09375, ((0, 16), (1, 8)))
    w_up = gaussian(key_of[6], (EXPERTS, FF, D), D ** -0.5, 0.09375, ((0, 16), (1, 8)))
    w_down = gaussian(key_of[7], (EXPERTS, FF, D), FF ** -0.5, 0.15625, ((0, 16), (1, 8)))
    return {"hidden_in": hidden_in, "block_output_gradient": block_output_gradient, "rms_norm_gain": rms_norm_gain, "routes": routes, "route_weights": route_weights, "w_gate": w_gate, "w_up": w_up, "w_down": w_down}


EPS = 1e-06

def place(blocks, cap, count):
    nb = blocks.shape[0]
    onehot = (blocks[..., None] == jnp.arange(count, dtype=jnp.int32)).astype(jnp.int32)
    before = lax.optimization_barrier(jnp.sum((jnp.cumsum(onehot, axis=1) - onehot) * onehot, axis=-1))
    return blocks * (nb * cap) + jnp.arange(nb, dtype=jnp.int32)[:, None] * cap + before

def expert_backward(inputs):
    rows_h, rows_dy, rows_w, gate_w, up_w, down_w = inputs
    gate = jnp.dot(rows_h, gate_w.T, preferred_element_type=jnp.float32)
    up = jnp.dot(rows_h, up_w.T, preferred_element_type=jnp.float32)
    back = jnp.dot(rows_dy, down_w.T, preferred_element_type=jnp.float32)
    sig = jax.nn.sigmoid(gate)
    silu = gate * sig
    act = silu * up
    weight = rows_w.astype(jnp.float32)[:, None]
    dact = weight * back
    dgate = (dact * up * sig * (1.0 + gate * (1.0 - sig))).astype(jnp.bfloat16)
    dup = (dact * silu).astype(jnp.bfloat16)
    actw = (weight * act).astype(jnp.bfloat16)
    width = FF // N_TENSOR
    part_h = jnp.zeros(rows_h.shape, jnp.float32)
    part_w = jnp.zeros(rows_h.shape[:1], jnp.float32)
    for piece in range(N_TENSOR):
        lo = piece * width
        hi = lo + width
        term = jnp.dot(dgate[:, lo:hi], gate_w[lo:hi], preferred_element_type=jnp.float32)
        term = term + jnp.dot(dup[:, lo:hi], up_w[lo:hi], preferred_element_type=jnp.float32)
        part_h = part_h + term.astype(jnp.bfloat16).astype(jnp.float32)
        inner = lax.optimization_barrier(jnp.sum(act[:, lo:hi] * back[:, lo:hi], axis=-1))
        part_w = part_w + inner.astype(jnp.bfloat16).astype(jnp.float32)
    grad_g = jnp.dot(dgate.T, rows_h, preferred_element_type=jnp.float32).astype(jnp.bfloat16)
    grad_u = jnp.dot(dup.T, rows_h, preferred_element_type=jnp.float32).astype(jnp.bfloat16)
    grad_d = jnp.dot(actw.T, rows_dy, preferred_element_type=jnp.float32).astype(jnp.bfloat16)
    return (part_h, part_w, grad_g, grad_u, grad_d)

def reference(hidden_in, block_output_gradient, rms_norm_gain, routes, route_weights, w_gate, w_up, w_down):
    devices = N_DP * N_TENSOR
    expert_values = hidden_in.astype(jnp.float32)
    inverse_rms_scale = lax.rsqrt(lax.optimization_barrier(jnp.mean(expert_values * expert_values, axis=-1, keepdims=True)) + EPS)
    unit_scaled_input = expert_values * inverse_rms_scale
    normalized_input = (unit_scaled_input * rms_norm_gain).astype(jnp.bfloat16)
    slots = CAP * devices
    flat = place(routes.reshape(devices, TOK_DEV * ROUTES), CAP, EXPERTS).reshape(-1)
    token_of = jnp.arange(TOKENS * ROUTES, dtype=jnp.int32) // ROUTES
    hbuf = jnp.zeros((EXPERTS * slots, D), jnp.bfloat16).at[flat].set(normalized_input[token_of])
    dybuf = jnp.zeros((EXPERTS * slots, D), jnp.bfloat16).at[flat].set(block_output_gradient[token_of])
    wbuf = jnp.zeros((EXPERTS * slots,), jnp.bfloat16).at[flat].set(route_weights.reshape(-1))
    part_h, part_w, grad_g, grad_u, grad_d = lax.map(expert_backward, (hbuf.reshape(EXPERTS, slots, D), dybuf.reshape(EXPERTS, slots, D), wbuf.reshape(EXPERTS, slots), w_gate, w_up, w_down))
    normalized_input_gradient = lax.optimization_barrier(jnp.sum(part_h.reshape(EXPERTS * slots, D)[flat].reshape(TOKENS, ROUTES, D), axis=1))
    grad_routes = part_w.reshape(-1)[flat].reshape(TOKENS, ROUTES)
    norm_gain_gradient = lax.optimization_barrier(jnp.sum(normalized_input_gradient * unit_scaled_input, axis=0))
    unit_input_gradient = normalized_input_gradient * rms_norm_gain
    expert_mixture = lax.optimization_barrier(jnp.mean(unit_input_gradient * unit_scaled_input, axis=-1, keepdims=True))
    block_input_gradient = (block_output_gradient.astype(jnp.float32) + inverse_rms_scale * (unit_input_gradient - unit_scaled_input * expert_mixture)).astype(jnp.bfloat16)
    return (block_input_gradient, norm_gain_gradient, grad_routes, grad_g, grad_u, grad_d)
```

```python
import jax
import jax.numpy as jnp
import numpy as np
from jax import lax
from jax.experimental import pallas as pl
from jax.experimental.pallas import tpu as pltpu
from jax.sharding import PartitionSpec as P

EPS = 1e-06
TOK = 128
D = 4096
CAP = 6
N_DP = 16
SLICE = 192
ROWS = N_DP * CAP
ALL = 8 * ROWS
WIDE_A = 2304
WIDE_B = D - WIDE_A
EXTRA = 256
CHUNK = 256
STEP = 1024
VMEM = 56 * 1024 * 1024
F32 = jnp.float32
BF16 = jnp.bfloat16


def params():
    return pltpu.CompilerParams(vmem_limit_bytes=VMEM)


def whole(shape):
    return pl.BlockSpec(shape, lambda *_: (0,) * len(shape))


def dot(a, b):
    return jnp.dot(a, b, preferred_element_type=F32)


def dot_nt(a, b):
    return lax.dot_general(a, b, (((1,), (1,)), ((), ())), preferred_element_type=F32)


def iota(shape, dim):
    return lax.broadcasted_iota(jnp.int32, shape, dim)


def dispatch_kernel(h_ref, c_ref, gain_ref, rcol_ref, rrow_ref, w_ref, out_ref, scale_ref, pick_ref):
    @pl.when(pl.program_id(0) == 0)
    def _():
        x = h_ref[...].astype(F32)
        scale_ref[...] = lax.rsqrt(jnp.mean(x * x, axis=-1, keepdims=True) + EPS)
        same = rcol_ref[...] == rrow_ref[...]
        earlier = iota((TOK, TOK), 0) < iota((TOK, TOK), 1)
        rank = jnp.sum(jnp.where(same & earlier, 1, 0), axis=0, keepdims=True)
        expert = rrow_ref[...]
        slot = (expert >> 1) * (4 * CAP) + (expert & 1) * CAP + rank
        rows = iota((N_DP * 4 * CAP, TOK), 0)
        pick_ref[:, :TOK] = jnp.where(rows == slot, 1.0, 0.0).astype(BF16)
        pick_ref[:, TOK:] = jnp.where(rows == slot + 2 * CAP, 1.0, 0.0).astype(BF16)

    cols = pl.ds(pl.multiple_of(pl.program_id(0) * 512, 512), 512)
    v = (h_ref[:, cols].astype(F32) * scale_ref[...] * gain_ref[...]).astype(BF16)
    c = (c_ref[:, cols].astype(F32) * w_ref[...].astype(F32)).astype(BF16)
    out_ref[...] = dot(pick_ref[...], jnp.concatenate([v, c], axis=0)).astype(BF16)


def dispatch(h, c, gain, rcol, rrow, w):
    rows = N_DP * 4 * CAP
    return pl.pallas_call(
        dispatch_kernel,
        grid=(D // 512,),
        in_specs=[
            whole((TOK, D)),
            whole((TOK, D)),
            pl.BlockSpec((1, 512), lambda j: (0, j)),
            whole((TOK, 1)),
            whole((1, TOK)),
            whole((TOK, 1)),
        ],
        out_specs=pl.BlockSpec((rows, 512), lambda j: (0, j)),
        out_shape=jax.ShapeDtypeStruct((rows, D), BF16),
        scratch_shapes=[pltpu.VMEM((TOK, 1), F32), pltpu.VMEM((rows, 2 * TOK), BF16)],
        compiler_params=params(),
        name="dispatch",
    )(h, c, gain, rcol, rrow, w)


def sort_matrix():
    out = np.zeros((4 * ROWS, 4 * ROWS), np.float32)
    for kind in range(4):
        for src in range(N_DP):
            for k in range(CAP):
                out[kind * ROWS + src * CAP + k, src * 4 * CAP + kind * CAP + k] = 1.0
    return out


def sort_kernel(m_ref, x_ref, *outs):
    for kind, out in enumerate(outs):
        rows = m_ref[kind * ROWS : (kind + 1) * ROWS, :]
        out[...] = dot(rows, x_ref[...]).astype(BF16)


def sort_rows(x):
    n = 4 * ROWS
    return pl.pallas_call(
        sort_kernel,
        grid=(D // 512,),
        in_specs=[whole((n, n)), pl.BlockSpec((n, 512), lambda j: (0, j))],
        out_specs=[pl.BlockSpec((ROWS, 512), lambda j: (0, j))] * 4,
        out_shape=[jax.ShapeDtypeStruct((ROWS, D), BF16)] * 4,
        compiler_params=params(),
        name="sort_rows",
    )(jnp.asarray(sort_matrix(), BF16), x)


def up(x):
    return lax.ppermute(x, "tensor", [(t, t // 4 * 4 + (t + 1) % 4) for t in range(8)])


def down(x):
    return lax.ppermute(x, "tensor", [(t, t // 4 * 4 + (t + 3) % 4) for t in range(8)])


def over(x):
    return lax.ppermute(x, "tensor", [(t, (t + 4) % 8) for t in range(8)])


def gather_z_first(h):
    hz = over(h)
    h1, h3 = up(h), down(h)
    z1, z3 = up(hz), down(hz)
    return [h, h1, up(h1), h3, hz, z1, down(z3), z3]


def gather_y_first(c, mirror):
    c1, c3 = up(c), down(c)
    c2 = down(c3) if mirror else up(c1)
    near = [c, c1, c2, c3]
    return near + [over(x) for x in near]


def add(a, b):
    return (a.astype(F32) + b.astype(F32)).astype(BF16)


def reduce_y(q, mirror):
    if mirror:
        return q[0], down(add(q[1], down(q[2]))), up(q[3])
    return q[0], up(add(q[3], up(q[2]))), down(q[1])


def reduce_y_first(p):
    near = reduce_y(p[:4], False)
    a, b, c = reduce_y(p[4:], True)
    far = (a.astype(F32) + b.astype(F32) + c.astype(F32)).astype(BF16)
    return near + (over(far),)


def reduce_z_first(p, mirror):
    return reduce_y([add(p[k], over(p[4 + k])) for k in range(4)], mirror)


def rows_kernel(*refs):
    hs, cs = refs[:8], refs[8:16]
    gate_ref, up_ref, down_ref, gate2_ref, up2_ref = refs[16:21]
    outs_a, outs_b = refs[21:29], refs[29:37]
    dgu_t_ref, act_t_ref = refs[37:39]
    acc_g, acc_u, acc_b, dgu_ref, pw_ref = refs[39:]
    s = pl.program_id(0)
    first = D // STEP
    n_a = WIDE_A // CHUNK
    n_b = WIDE_B // CHUNK

    @pl.when(s < first)
    def _():
        h = jnp.concatenate([r[...] for r in hs], axis=0)
        c = jnp.concatenate([r[...] for r in cs], axis=0)
        g = dot_nt(h, gate_ref[0])
        u = dot_nt(h, up_ref[0])
        b = dot_nt(c, down_ref[0])

        @pl.when(s == 0)
        def _():
            acc_g[...] = g
            acc_u[...] = u
            acc_b[...] = b

        @pl.when(s > 0)
        def _():
            acc_g[...] += g
            acc_u[...] += u
            acc_b[...] += b

    @pl.when(s == first - 1)
    def _():
        gate, upp, back = acc_g[...], acc_u[...], acc_b[...]
        sig = jax.nn.sigmoid(gate)
        silu = gate * sig
        act = silu * upp
        dgate = back * upp * sig * (1.0 + gate * (1.0 - sig))
        dup = back * silu
        dgu_ref[:, :SLICE] = dgate.astype(BF16)
        dgu_ref[:, SLICE:] = dup.astype(BF16)
        dgu_t_ref[:SLICE, :] = dgate.T.astype(BF16)
        dgu_t_ref[SLICE:, :] = dup.T.astype(BF16)
        act_t_ref[...] = act.T.astype(BF16)
        pw_ref[...] = jnp.sum(act * back, axis=-1, keepdims=True)

    def part():
        w = jnp.concatenate([gate2_ref[0], up2_ref[0]], axis=0)
        return dot(dgu_ref[...], w).astype(BF16)

    def put(outs, value):
        for k, out in enumerate(outs):
            out[...] = value[k * ROWS : (k + 1) * ROWS]

    @pl.when((s >= first) & (s < first + n_a))
    def _():
        put(outs_a, part())

    @pl.when((s >= first + n_a) & (s < first + n_a + n_b))
    def _():
        put(outs_b, part())

    @pl.when(s == first + n_a + n_b)
    def _():
        pw = pw_ref[...]
        high = pw.astype(BF16).astype(F32)
        lane = iota((ALL, EXTRA), 1)
        value = jnp.where(lane == 0, high, jnp.where(lane == 1, pw - high, 0.0))
        put(outs_b, value.astype(BF16))


def expert_rows(e, hs, cs, w_gate, w_up, w_down):
    first = D // STEP
    n_a = WIDE_A // CHUNK
    n_b = WIDE_B // CHUNK
    n = n_a + n_b
    head = lambda s: jnp.minimum(s, first - 1)
    tail = lambda s: jnp.clip(s - first, 0, n - 1)
    rows = pl.BlockSpec((ROWS, STEP), lambda s: (0, head(s)))
    weight = pl.BlockSpec((1, SLICE, STEP), lambda s: (e, 0, head(s)))
    again = pl.BlockSpec((1, SLICE, CHUNK), lambda s: (e, 0, tail(s)))
    out_a = pl.BlockSpec((ROWS, CHUNK), lambda s: (0, jnp.clip(s - first, 0, n_a - 1)))
    out_b = pl.BlockSpec((ROWS, CHUNK), lambda s: (0, jnp.clip(s - first - n_a, 0, n_b)))
    out = pl.pallas_call(
        rows_kernel,
        grid=(first + n + 1,),
        in_specs=[rows] * 16 + [weight] * 3 + [again] * 2,
        out_specs=[out_a] * 8 + [out_b] * 8 + [whole((2 * SLICE, ALL)), whole((SLICE, ALL))],
        out_shape=[jax.ShapeDtypeStruct((ROWS, WIDE_A), BF16)] * 8
        + [jax.ShapeDtypeStruct((ROWS, WIDE_B + EXTRA), BF16)] * 8
        + [jax.ShapeDtypeStruct((2 * SLICE, ALL), BF16), jax.ShapeDtypeStruct((SLICE, ALL), BF16)],
        scratch_shapes=[
            pltpu.VMEM((ALL, SLICE), F32),
            pltpu.VMEM((ALL, SLICE), F32),
            pltpu.VMEM((ALL, SLICE), F32),
            pltpu.VMEM((ALL, 2 * SLICE), BF16),
            pltpu.VMEM((ALL, 1), F32),
        ],
        compiler_params=params(),
        cost_estimate=pl.CostEstimate(
            flops=2 * ALL * SLICE * D * 5, bytes_accessed=26 << 20, transcendentals=ALL * SLICE
        ),
        name="expert_rows",
    )(*hs, *cs, w_gate, w_up, w_down, w_gate, w_up)
    return out[:8], out[8:16], out[16], out[17]


def weights_kernel(*refs):
    hs, cs = refs[:8], refs[8:16]
    dgu_t_ref, act_t_ref, gate_ref, up_ref = refs[16:20]
    gg_ref, gu_ref, gd_ref, norm_ref = refs[-4:]
    h = jnp.concatenate([r[...] for r in hs], axis=0)
    c = jnp.concatenate([r[...] for r in cs], axis=0)
    gu = dot(dgu_t_ref[...], h)
    gg_ref[0] = gu[:SLICE].astype(BF16)
    gu_ref[0] = gu[SLICE:].astype(BF16)
    gd_ref[0] = dot(act_t_ref[...], c).astype(BF16)
    norm = gu[:SLICE] * gate_ref[0].astype(F32) + gu[SLICE:] * up_ref[0].astype(F32)
    norm_ref[...] = jnp.sum(norm, axis=0, keepdims=True)


def expert_weights(e, hs, cs, dgu_t, act_t, w_gate, w_up, before):
    rows = pl.BlockSpec((ROWS, 512), lambda j: (0, j))
    weight = pl.BlockSpec((1, SLICE, 512), lambda j: (e, 0, j))
    grad = jax.ShapeDtypeStruct((2, SLICE, D), BF16)
    return pl.pallas_call(
        weights_kernel,
        grid=(D // 512,),
        in_specs=[rows] * 16
        + [whole((2 * SLICE, ALL)), whole((SLICE, ALL)), weight, weight]
        + [pl.BlockSpec(memory_space=pl.ANY)] * len(before),
        out_specs=[weight] * 3 + [pl.BlockSpec((1, 512), lambda j: (0, j))],
        out_shape=[grad] * 3 + [jax.ShapeDtypeStruct((1, D), F32)],
        input_output_aliases={20 + k: k for k in range(len(before))},
        compiler_params=params(),
        cost_estimate=pl.CostEstimate(
            flops=2 * ALL * SLICE * D * 3, bytes_accessed=18 << 20, transcendentals=0
        ),
        name="expert_weights",
    )(*hs, *cs, dgu_t, act_t, w_gate, w_up, *before)


def pack_matrices():
    rows = np.zeros((N_DP * 16, 2 * ROWS), np.float32)
    lanes = np.zeros((2 * ROWS, 128), np.float32)
    high = np.zeros((N_DP * 16, 2 * ROWS), np.float32)
    low = np.zeros((N_DP * 16, 2 * ROWS), np.float32)
    for e in range(2):
        for src in range(N_DP):
            for k in range(CAP):
                s = e * ROWS + src * CAP + k
                rows[src * 16 + e * CAP + k, s] = 1.0
                lanes[s, e * CAP + k] = 1.0
                high[src * 16 + 2 * CAP, s] = 1.0
                low[src * 16 + 2 * CAP + 1, s] = 1.0
    return rows, lanes, high, low


def pack_kernel(*refs):
    rows_ref, lanes_ref, high_ref, low_ref = refs[:4]
    a0, a1, b0, b1 = refs[4:8], refs[8:12], refs[12:15], refs[15:18]
    out_ref = refs[18]

    def total(parts, cols):
        value = parts[0][:, cols].astype(F32)
        for p in parts[1:]:
            value = value + p[:, cols].astype(F32)
        return value

    def both(first, second, cols):
        return jnp.concatenate([total(first, cols), total(second, cols)], axis=0)

    rows = rows_ref[...]
    for j in range(WIDE_A // CHUNK):
        cols = slice(j * CHUNK, (j + 1) * CHUNK)
        out_ref[:, cols] = dot(rows, both(a0, a1, cols).astype(BF16)).astype(BF16)
    for j in range(WIDE_B // CHUNK):
        cols = slice(j * CHUNK, (j + 1) * CHUNK)
        value = dot(rows, both(b0, b1, cols).astype(BF16)).astype(BF16)
        out_ref[:, WIDE_A + j * CHUNK : WIDE_A + (j + 1) * CHUNK] = value
    pw = both(b0, b1, slice(WIDE_B, WIDE_B + 128))
    pw = pw[:, 0:1] + pw[:, 1:2]
    top = pw.astype(BF16).astype(F32)
    spread = lanes_ref[...].astype(F32)
    value = dot(high_ref[...], (top * spread).astype(BF16))
    value = value + dot(low_ref[...], ((pw - top) * spread).astype(BF16))
    out_ref[:, :128] = (out_ref[:, :128].astype(F32) + value).astype(BF16)


def pack(a0, a1, b0, b1):
    mats = [jnp.asarray(m, BF16) for m in pack_matrices()]
    return pl.pallas_call(
        pack_kernel,
        out_shape=jax.ShapeDtypeStruct((N_DP * 16, D), BF16),
        compiler_params=params(),
        name="pack_rows",
    )(*mats, *a0, *a1, *b0, *b1)


def combine_kernel(r_ref, h_ref, c_ref, gain_ref, rcol_ref, rrow_ref, w_ref, out_ref, routes_ref):
    same = rcol_ref[...] == rrow_ref[...]
    earlier = iota((TOK, TOK), 1) < iota((TOK, TOK), 0)
    rank = jnp.sum(jnp.where(same & earlier, 1, 0), axis=1, keepdims=True)
    expert = rcol_ref[...]
    place = (expert & 1) * CAP + rank
    base = (expert >> 1) * 16
    cols = iota((TOK, N_DP * 16), 1)

    def choose(index):
        return jnp.where(cols == index, 1.0, 0.0).astype(BF16)

    pw = dot(choose(base + 2 * CAP), r_ref[:, :128]) + dot(choose(base + 2 * CAP + 1), r_ref[:, :128])
    pw = jnp.sum(jnp.where(iota((TOK, 128), 1) == place, pw, 0.0), axis=1, keepdims=True)
    routes_ref[...] = pw / w_ref[...].astype(F32)
    g = dot(choose(base + place), r_ref[...])
    x = h_ref[...].astype(F32)
    scale = lax.rsqrt(jnp.mean(x * x, axis=-1, keepdims=True) + EPS)
    x = x * scale
    dx = g * gain_ref[...]
    mix = jnp.mean(dx * x, axis=-1, keepdims=True)
    out_ref[...] = (c_ref[...].astype(F32) + scale * (dx - x * mix)).astype(BF16)


def combine(r, h, c, gain, rcol, rrow, w):
    return pl.pallas_call(
        combine_kernel,
        out_shape=[
            jax.ShapeDtypeStruct((TOK, D), BF16),
            jax.ShapeDtypeStruct((TOK, 1), F32),
        ],
        compiler_params=params(),
        name="combine",
    )(r, h, c, gain, rcol, rrow, w)


def body(h, c, gain, routes, w, w_gate, w_up, w_down):
    gain = gain.reshape(1, D)
    rrow = routes.reshape(1, TOK)
    slots = dispatch(h, c, gain, routes, rrow, w)
    got = lax.all_to_all(
        slots.reshape(N_DP, 4 * CAP, D), "dp", split_axis=0, concat_axis=0, tiled=True
    )
    h0, h1, c0, c1 = sort_rows(got.reshape(4 * ROWS, D))
    hs0, cs0 = gather_z_first(h0), gather_y_first(c0, False)
    hs1, cs1 = gather_z_first(h1), gather_y_first(c1, True)
    pa0, pb0, dgu0, act0 = expert_rows(0, hs0, cs0, w_gate, w_up, w_down)
    pa1, pb1, dgu1, act1 = expert_rows(1, hs1, cs1, w_gate, w_up, w_down)
    a0, b0 = reduce_y_first(pa0), reduce_z_first(pb0, False)
    a1, b1 = reduce_y_first(pa1), reduce_z_first(pb1, True)
    *grads, norm0 = expert_weights(0, hs0, cs0, dgu0, act0, w_gate, w_up, ())
    gg, gu, gd, norm1 = expert_weights(1, hs1, cs1, dgu1, act1, w_gate, w_up, grads)
    norm = lax.psum(((norm0 + norm1) / gain).reshape(D), ("dp", "tensor"))
    packed = pack(a0, a1, b0, b1)
    back = lax.all_to_all(packed.reshape(N_DP, 16, D), "dp", split_axis=0, concat_axis=0, tiled=True)
    out, grad_routes = combine(back.reshape(N_DP * 16, D), h, c, gain, routes, rrow, w)
    return out, norm, grad_routes, gg, gu, gd


def solution(mesh):
    tokens = P(("dp", "tensor"), None)
    weights = P("dp", "tensor", None)
    return jax.shard_map(
        body,
        mesh=mesh,
        in_specs=(tokens, tokens, P(), tokens, tokens, weights, weights, weights),
        out_specs=(tokens, P(), tokens, weights, weights, weights),
        check_vma=False,
    )
```

```python
import functools

import jax
import jax.numpy as jnp
import numpy as np
from jax import lax
from jax.experimental import pallas as pl
from jax.experimental.pallas import tpu as pltpu
from jax.sharding import PartitionSpec as P

EPS = 1e-06
TOK = 128
D = 4096
HALF = D // 2
QUART = D // 4
CAP = 6
N_DP = 16
SLICE = 192
ROWS = N_DP * CAP
PART = 4 * ROWS
EXTRA = 128
VMEM = 56 * 1024 * 1024
F32 = jnp.float32
BF16 = jnp.bfloat16


def params():
    return pltpu.CompilerParams(vmem_limit_bytes=VMEM)


def whole(shape):
    return pl.BlockSpec(shape, lambda *_: (0,) * len(shape))


def dot(a, b):
    return jnp.dot(a, b, preferred_element_type=F32)


def dot_nt(a, b):
    return lax.dot_general(a, b, (((1,), (1,)), ((), ())), preferred_element_type=F32)


def iota(shape, dim):
    return lax.broadcasted_iota(jnp.int32, shape, dim)


def stack(refs, cols=slice(None)):
    return jnp.concatenate([r[:, cols] for r in refs], axis=0)


def move(i, kind):
    z, y = divmod(i % 8, 4)
    if kind == "z":
        z = z ^ 1
    elif (kind == "trade") == (i // 8 % 2 == 0):
        y = y ^ 1
    else:
        y = 3 - y
    return i // 8 * 8 + z * 4 + y


AXES = ("dp", "tensor")
PERMS = {k: [(i, move(i, k)) for i in range(128)] for k in ("trade", "y", "z")}


def trade(x):
    return lax.ppermute(x, AXES, PERMS["trade"])


def trade_for(core, x):
    return lax.ppermute(x, "tensor", [(t, move(core * 8 + t, "trade") % 8) for t in range(8)])


def over_y(x):
    return lax.ppermute(x, AXES, PERMS["y"])


def over_z(x):
    return lax.ppermute(x, AXES, PERMS["z"])


def owned():
    y = lax.axis_index("tensor") & 3
    return jnp.where((y == 0) | (y == 3), 1, 0).astype(jnp.int32), y >> 1


def column(row):
    diagonal = iota((TOK, TOK), 0) == iota((TOK, TOK), 1)
    return jnp.sum(jnp.where(diagonal, row, jnp.zeros_like(row)), axis=1, keepdims=True)


def rank_of(rrow, axis):
    same = column(rrow) == rrow
    earlier = iota((TOK, TOK), axis) < iota((TOK, TOK), 1 - axis)
    return jnp.sum(jnp.where(same & earlier, 1, 0), axis=axis, keepdims=True)


def place_of(expert, own_ref):
    dp = expert >> 1
    mine = jnp.where((dp & 1) == 0, own_ref[0], own_ref[1])
    return dp, (expert & 1) ^ mine


def dispatch_kernel(turn, own_ref, h_ref, c_ref, gain_ref, rrow_ref, wrow_ref, *outs):
    rows = 4 * ROWS
    len_out = rows // len(outs)
    x = h_ref[...].astype(F32)
    scale = lax.rsqrt(jnp.mean(x * x, axis=-1, keepdims=True) + EPS)
    weight = column(wrow_ref[...].astype(F32))
    rank = rank_of(rrow_ref[...], 0)
    dp, when = place_of(rrow_ref[...], own_ref)
    if len(outs) == 2:
        dp = (dp >> 1) + (dp & 1) * (N_DP // 2)
    slot = jnp.where(when == turn, dp * (4 * CAP) + rank, -4 * CAP)
    at = iota((rows, TOK), 0)
    pick = [jnp.where(at == slot + k * CAP, 1.0, 0.0).astype(BF16) for k in range(4)]
    pick = jnp.concatenate(pick, axis=1)
    wide = 512
    for j in range(HALF // wide):
        value = []
        for half in range(2):
            cols = slice(half * HALF + j * wide, half * HALF + (j + 1) * wide)
            value.append((x[:, cols] * scale * gain_ref[:, cols]).astype(BF16))
            value.append((c_ref[:, cols].astype(F32) * weight).astype(BF16))
        rows_j = dot(pick, jnp.concatenate(value, axis=0)).astype(BF16)
        for k, out in enumerate(outs):
            out[:, j * wide : (j + 1) * wide] = rows_j[k * len_out : (k + 1) * len_out]


def dispatch(turn, own, h, c, gain, rrow, wrow):
    return pl.pallas_call(
        functools.partial(dispatch_kernel, turn),
        in_specs=[pl.BlockSpec(memory_space=pltpu.SMEM)] + [pl.BlockSpec(memory_space=pltpu.VMEM)] * 5,
        out_shape=[jax.ShapeDtypeStruct((4 * ROWS // (1 + turn), HALF), BF16)] * (1 + turn),
        compiler_params=params(),
        cost_estimate=pl.CostEstimate(flops=2 * 384 * 512 * HALF, bytes_accessed=4 << 20, transcendentals=0),
        name="dispatch",
    )(own, h, c, gain, rrow, wrow)


def sort_matrix():
    out = np.zeros((4 * ROWS, 4 * ROWS), np.float32)
    for block in range(4):
        for src in range(N_DP):
            for k in range(CAP):
                out[block * ROWS + src * CAP + k, src * 4 * CAP + block * CAP + k] = 1.0
    return out


def sort_kernel(m_ref, x_ref, out_ref):
    for half in range(2):
        rows = m_ref[half * 2 * ROWS : (half + 1) * 2 * ROWS, :]
        out_ref[:, half * HALF : (half + 1) * HALF] = dot(rows, x_ref[...]).astype(BF16)


def sort_rows(x):
    return pl.pallas_call(
        sort_kernel,
        out_shape=jax.ShapeDtypeStruct((2 * ROWS, D), BF16),
        compiler_params=params(),
        cost_estimate=pl.CostEstimate(flops=2 * 384 * 384 * HALF, bytes_accessed=4 << 20, transcendentals=0),
        name="sort_rows",
    )(jnp.asarray(sort_matrix(), BF16), x)


def tie(x, *others):
    return barrier(x, *others)[0]


def barrier(*arrays):
    return list(lax.optimization_barrier(arrays))


def pieces(hs, cs, wide):
    specs = [pl.BlockSpec((ROWS, wide), lambda s, own, k=k: (k, s)) for _, k in hs + cs]
    return specs, [x for x, _ in hs + cs]


def slices(count, wide):
    return [pl.BlockSpec((SLICE, wide), lambda s, own, k=k: (k, s)) for k in range(count)]


def add(a, b):
    return (a.astype(F32) + b.astype(F32)).astype(BF16)


def sum_dp(x, bit):
    return x + lax.ppermute(x, "dp", [(i, i ^ bit) for i in range(16)])


def spread(x):
    return jnp.where(iota((8, D), 0) == lax.axis_index("tensor"), x, 0.0)


def forward_kernel(own_ref, *refs):
    hs, cs = refs[:4], refs[4:8]
    gate_ref, up_ref, down_ref, gate2_ref, up2_ref, down2_ref = refs[8:14]
    dgu_ref, dgu_t_ref, act_t_ref, pw_ref = refs[14:18]
    acc_g, acc_u, acc_b = refs[18:]
    s = pl.program_id(0)
    h, c = stack(hs), stack(cs)
    g = dot_nt(h, jnp.concatenate([gate_ref[0], gate2_ref[...]], axis=0))
    u = dot_nt(h, jnp.concatenate([up_ref[0], up2_ref[...]], axis=0))
    b = dot_nt(c, jnp.concatenate([down_ref[0], down2_ref[...]], axis=0))

    @pl.when(s == 0)
    def _():
        acc_g[...] = g
        acc_u[...] = u
        acc_b[...] = b

    @pl.when(s > 0)
    def _():
        acc_g[...] += g
        acc_u[...] += u
        acc_b[...] += b

    @pl.when(s == pl.num_programs(0) - 1)
    def _():
        gate, upp, back = acc_g[...], acc_u[...], acc_b[...]
        sig = jax.nn.sigmoid(gate)
        silu = gate * sig
        act = silu * upp
        dgate = back * upp * sig * (1.0 + gate * (1.0 - sig))
        dup = back * silu
        for part in range(2):
            cols = slice(part * SLICE, (part + 1) * SLICE)
            lo = part * 2 * SLICE
            dgu_ref[:, lo : lo + SLICE] = dgate[:, cols].astype(BF16)
            dgu_ref[:, lo + SLICE : lo + 2 * SLICE] = dup[:, cols].astype(BF16)
        dgate_t, dup_t = dgate.T.astype(BF16), dup.T.astype(BF16)
        for part in range(2):
            rows = slice(part * SLICE, (part + 1) * SLICE)
            lo = part * 2 * SLICE
            dgu_t_ref[lo : lo + SLICE, :] = dgate_t[rows]
            dgu_t_ref[lo + SLICE : lo + 2 * SLICE, :] = dup_t[rows]
        act_t_ref[...] = act.T.astype(BF16)
        pw = jnp.sum(act * back, axis=-1, keepdims=True)
        high = pw.astype(BF16).astype(F32)
        lane = iota((PART, EXTRA), 1)
        value = jnp.where(lane == 0, high, jnp.where(lane == 1, pw - high, 0.0))
        pw_ref[...] = value.astype(BF16)


def forward(own, hs, cs, weights, got_gu, got_d):
    step = 1024
    specs, arrays = pieces(hs, cs, step)
    mine = pl.BlockSpec((1, SLICE, step), lambda s, own: (own[0], 0, s))
    shapes = [(PART, 4 * SLICE), (4 * SLICE, PART), (2 * SLICE, PART), (PART, EXTRA)]
    return pl.pallas_call(
        forward_kernel,
        grid_spec=pltpu.PrefetchScalarGridSpec(
            num_scalar_prefetch=1,
            grid=(D // step,),
            in_specs=specs + [mine] * 3 + slices(2, step) + slices(1, step),
            out_specs=[whole(s) for s in shapes],
            scratch_shapes=[pltpu.VMEM((PART, 2 * SLICE), F32)] * 3,
        ),
        out_shape=[jax.ShapeDtypeStruct(s, BF16) for s in shapes],
        compiler_params=params(),
        cost_estimate=pl.CostEstimate(
            flops=2 * PART * 6 * SLICE * D, bytes_accessed=16 << 20, transcendentals=PART * 384
        ),
        name="expert_forward",
    )(own, *arrays, *weights, got_gu, got_gu, got_d)


def rows_kernel(own_ref, dgu_ref, pw_ref, *refs):
    hs = refs[:4]
    gate_ref, up_ref, gate2_ref, up2_ref = refs[4:8]
    outs, norm_ref = refs[8:12], refs[12]
    s = pl.program_id(0)
    wide = gate_ref.shape[-1]
    w = jnp.concatenate([gate_ref[0], up_ref[0], gate2_ref[...], up2_ref[...]], axis=0)
    value = dot(dgu_ref[...], w)
    norm_ref[...] = jnp.sum(value * stack(hs).astype(F32), axis=0, keepdims=True)
    value = value.astype(BF16)
    cols = pl.ds(pl.multiple_of(s * wide, wide), wide)
    for k, out in enumerate(outs):
        out[:, cols] = value[k * ROWS : (k + 1) * ROWS]

    @pl.when(s == 0)
    def _():
        for k, out in enumerate(outs):
            out[:, D:] = pw_ref[k * ROWS : (k + 1) * ROWS, :]


def expert_rows(own, dgu, pw, hs, weights, got):
    wide = 512
    mine = pl.BlockSpec((1, SLICE, wide), lambda s, own: (own[0], 0, s))
    specs, arrays = pieces(hs, [], wide)
    shape = (ROWS, D + EXTRA)
    return pl.pallas_call(
        rows_kernel,
        grid_spec=pltpu.PrefetchScalarGridSpec(
            num_scalar_prefetch=1,
            grid=(D // wide,),
            in_specs=[whole((PART, 4 * SLICE)), whole((PART, EXTRA))] + specs + [mine, mine] + slices(2, wide),
            out_specs=[whole(shape)] * 4 + [pl.BlockSpec((1, wide), lambda s, own: (0, s))],
        ),
        out_shape=[jax.ShapeDtypeStruct(shape, BF16)] * 4 + [jax.ShapeDtypeStruct((1, D), F32)],
        compiler_params=params(),
        cost_estimate=pl.CostEstimate(
            flops=2 * PART * 4 * SLICE * D, bytes_accessed=10 << 20, transcendentals=0
        ),
        name="expert_rows",
    )(own, dgu, pw, *arrays, weights[0], weights[1], got, got)


def weights_kernel(part, kinds, own_ref, *refs):
    outs = refs[-len(kinds) :]
    hs, cs = refs[:8], refs[8:16]
    if 2 not in kinds:
        lhs, lo, hi, rows = refs[8:10], part * 2 + kinds[0], part * 2 + kinds[-1] + 1, hs
        values = dot(jnp.concatenate([r[lo * SLICE : hi * SLICE] for r in lhs], axis=1), stack(rows))
        values = [values[k * SLICE : (k + 1) * SLICE] for k in range(len(kinds))]
    elif kinds == (2,):
        lhs, rows = refs[8:10], hs
        values = [dot(jnp.concatenate([r[part * SLICE : (part + 1) * SLICE] for r in lhs], axis=1), stack(rows))]
    else:
        lo = part * 2 * SLICE
        lhs = [r[lo : lo + 2 * SLICE] for r in refs[16:18]]
        values = dot(jnp.concatenate(lhs, axis=1), stack(hs))
        values = [values[:SLICE], values[SLICE:]]
        lhs = [r[part * SLICE : (part + 1) * SLICE] for r in refs[18:20]]
        values.append(dot(jnp.concatenate(lhs, axis=1), stack(cs)))
    for out, value in zip(outs, values):
        if part == 0:
            out[0] = value.astype(BF16)
        else:
            out[...] = value.astype(BF16)


def expert_weights(part, kinds, own, hs, cs, dgu_t, act_t, after):
    wide = 512
    hs, dgu_t = (hs, dgu_t) if 0 in kinds or 1 in kinds else ([], ())
    cs, act_t = (cs, act_t) if 2 in kinds else ([], ())
    specs, arrays = pieces(hs, cs, wide)
    if part == 0:
        made = pl.BlockSpec((1, SLICE, wide), lambda j, own: (own[0], 0, j))
        grad = jax.ShapeDtypeStruct((2, SLICE, D), BF16)
    else:
        made = pl.BlockSpec((SLICE, wide), lambda j, own: (0, j))
        grad = jax.ShapeDtypeStruct((SLICE, D), BF16)
    out = pl.pallas_call(
        functools.partial(weights_kernel, part, kinds),
        grid_spec=pltpu.PrefetchScalarGridSpec(
            num_scalar_prefetch=1,
            grid=(D // wide,),
            in_specs=specs
            + [whole((4 * SLICE, PART))] * len(dgu_t)
            + [whole((2 * SLICE, PART))] * len(act_t)
            + [pl.BlockSpec(memory_space=pl.ANY)] * len(after),
            out_specs=[made] * len(kinds),
        ),
        out_shape=[grad] * len(kinds),
        compiler_params=params(),
        cost_estimate=pl.CostEstimate(
            flops=2 * 2 * PART * len(kinds) * SLICE * D, bytes_accessed=len(kinds) * 6 << 20, transcendentals=0
        ),
        name="expert_weights",
    )(own, *arrays, *dgu_t, *act_t, *after)
    return list(out)


def pack_matrix():
    out = np.zeros((4 * ROWS, 4 * ROWS), np.float32)
    for quarter in range(4):
        for src in range(N_DP):
            for k in range(CAP):
                out[src * 4 * CAP + quarter * CAP + k, quarter * ROWS + src * CAP + k] = 1.0
    return out


def pack_kernel(m_ref, p_ref, q_ref, r_ref, out_ref):
    def total(cols):
        return p_ref[:, cols].astype(F32) + q_ref[:, cols].astype(F32) + r_ref[:, cols].astype(F32)

    wide = 512
    for j in range(QUART // wide):
        lo = j * wide
        rows = [total(slice(q * QUART + lo, q * QUART + lo + wide)).astype(BF16) for q in range(4)]
        out_ref[:, lo : lo + wide] = dot(m_ref[...], jnp.concatenate(rows, axis=0)).astype(BF16)
    pw = total(slice(D, D + EXTRA))
    pw = pw[:, 0:1] + pw[:, 1:2]
    high = pw.astype(BF16).astype(F32)
    lane = iota((ROWS, EXTRA), 1)
    value = jnp.where(lane == 0, high, jnp.where(lane == 1, pw - high, 0.0)).astype(BF16)
    out_ref[:, QUART:] = dot(m_ref[:, :ROWS], value).astype(BF16)


def pack(p, q, r):
    return pl.pallas_call(
        pack_kernel,
        out_shape=jax.ShapeDtypeStruct((4 * ROWS, QUART + EXTRA), BF16),
        compiler_params=params(),
        cost_estimate=pl.CostEstimate(flops=2 * 384 * 384 * QUART, bytes_accessed=4 << 20, transcendentals=0),
        name="pack_rows",
    )(jnp.asarray(pack_matrix(), BF16), p, q, r)


def combine_kernel(own_ref, r0_ref, r1_ref, h_ref, c_ref, gain_ref, rrow_ref, wrow_ref, out_ref, routes_ref):
    rank = rank_of(rrow_ref[...], 1)
    dp, when = place_of(column(rrow_ref[...]), own_ref)
    place = dp * (4 * CAP) + rank + when * (4 * ROWS)
    at = iota((TOK, 8 * ROWS), 1)
    r = jnp.concatenate([r0_ref[...], r1_ref[...]], axis=0)
    picks = [jnp.where(at == place + q * CAP, 1.0, 0.0).astype(BF16) for q in range(4)]
    pw = dot(picks[0], r[:, QUART:])
    diagonal = iota((TOK, TOK), 0) == iota((TOK, TOK), 1)
    pw = jnp.sum(jnp.where(diagonal, pw[:, 0:1] + pw[:, 1:2], 0.0), axis=0, keepdims=True)
    routes_ref[...] = pw / wrow_ref[...].astype(F32)
    g = jnp.concatenate([dot(p, r[:, :QUART]) for p in picks], axis=1)
    x = h_ref[...].astype(F32)
    scale = lax.rsqrt(jnp.mean(x * x, axis=-1, keepdims=True) + EPS)
    x = x * scale
    dx = g * gain_ref[...]
    mix = jnp.mean(dx * x, axis=-1, keepdims=True)
    out_ref[...] = (c_ref[...].astype(F32) + scale * (dx - x * mix)).astype(BF16)


def combine(own, r0, r1, h, c, gain, rrow, wrow):
    return pl.pallas_call(
        combine_kernel,
        in_specs=[pl.BlockSpec(memory_space=pltpu.SMEM)] + [pl.BlockSpec(memory_space=pltpu.VMEM)] * 7,
        out_shape=[
            jax.ShapeDtypeStruct((TOK, D), BF16),
            jax.ShapeDtypeStruct((1, TOK), F32),
        ],
        compiler_params=params(),
        cost_estimate=pl.CostEstimate(flops=2 * 128 * 768 * D, bytes_accessed=5 << 20, transcendentals=0),
        name="combine",
    )(own, r0, r1, h, c, gain, rrow, wrow)


def exchange(x):
    shaped = x.reshape((N_DP, -1) + x.shape[1:])
    got = lax.all_to_all(shaped, "dp", split_axis=0, concat_axis=0, tiled=True)
    return got.reshape(x.shape)


def body(h, c, gain, routes, w, w_gate, w_up, w_down):
    gain = gain.reshape(1, D)
    rrow, wrow = routes.reshape(1, TOK), w.reshape(1, TOK)
    own0, own1 = owned()
    owns = jnp.stack([own0, own1])
    mine = jnp.where((lax.axis_index("dp") & 1) == 0, own0, own1)
    own = mine.reshape(1)
    weights = (w_gate, w_up, w_down)

    slots_a = dispatch(1, owns, h, c, gain, rrow, wrow)
    slots_a = [trade_for(core, x).reshape(N_DP // 2, -1, HALF) for core, x in enumerate(slots_a)]
    (slots_b,) = dispatch(0, owns, h, c, gain, rrow, wrow)
    leave = [lax.dynamic_index_in_dim(x, 1 - mine, 0, keepdims=False) for x in weights]
    leave_gu = jnp.concatenate(leave[:2], axis=0)
    *slots_a, slots_b, leave_gu = barrier(*slots_a, slots_b, leave_gu)
    got_a = exchange(jnp.stack(slots_a, axis=1).reshape(4 * ROWS, HALF))
    got_gu = trade(leave_gu)
    got_a, leave_d = barrier(got_a, leave[2])
    got_b = exchange(slots_b)
    a = sort_rows(got_a)
    got_d = trade(leave_d)
    az, ay = over_z(a), over_y(a)
    az, ay, got_b, got_gu = barrier(az, ay, got_b, got_gu)
    b = sort_rows(got_b)
    ao, bz, by = over_y(az), over_z(b), over_y(b)
    piece_a = (a, ay, az, ao)
    hs_a, cs_a = [(x, 0) for x in piece_a], [(x, 1) for x in piece_a]
    dgu_a, dgu_ta, act_ta, pw_a = forward(own, hs_a, cs_a, weights, got_gu, got_d)
    bz, by, dgu_a = barrier(bz, by, dgu_a)
    bo = over_y(bz)
    *pa, norm = expert_rows(own, dgu_a, pw_a, hs_a, weights, got_gu)
    za, ya = over_z(pa[3]), over_z(pa[2])

    piece_b = (b, by, bz, bo)
    hs_b, cs_b = [(x, 0) for x in piece_b], [(x, 1) for x in piece_b]
    dgu_b, dgu_tb, act_tb, pw_b = forward(own, hs_b, cs_b, weights, got_gu, got_d)
    dgu_b, za = barrier(dgu_b, za)
    fa = over_y(add(pa[1], za))
    *pb, norm_b = expert_rows(own, dgu_b, pw_b, hs_b, weights, got_gu)
    norm = (norm + norm_b) / gain
    hs, cs, dgu_t, act_t = hs_a + hs_b, cs_a + cs_b, (dgu_ta, dgu_tb), (act_ta, act_tb)
    grads = functools.partial(expert_weights, own=own, hs=hs, cs=cs, dgu_t=dgu_t, act_t=act_t)
    zb, yb = over_z(pb[3]), over_z(pb[2])
    packed_a = pack(tie(pa[0], pb[0]), ya, fa)
    (give_g,) = grads(1, (0,), after=(packed_a,))
    packed_a, give_g, norm = barrier(trade(packed_a), give_g, sum_dp(norm, 1))
    r_a = exchange(packed_a)
    (give_u,) = grads(1, (1,), after=(packed_a,))
    zb, give_u, norm = barrier(zb, give_u, sum_dp(norm, 2))
    far = add(pb[1], zb)
    fb = over_y(far)
    mine_gud = grads(0, (0, 1, 2), after=(far,))
    take_g, norm, mine_gud[0] = barrier(trade(give_g), sum_dp(norm, 4), mine_gud[0])
    (give_d,) = grads(1, (2,), after=(take_g,))
    yb, fb, norm, give_d = barrier(yb, fb, sum_dp(norm, 8), give_d)
    packed_b = pack(pb[0], yb, fb)
    norm = spread(norm)
    r_a, packed_b, take_u, norm = barrier(r_a, packed_b, trade(give_u), norm + over_z(norm))
    r_b = exchange(packed_b)
    take_d = trade(give_d)
    norm = norm + over_y(norm)
    norm = jnp.sum(norm + trade(norm), axis=0)
    out, grad_routes = combine(owns, r_b, r_a, h, c, gain, rrow, wrow)
    grad_routes = grad_routes.reshape(TOK, 1)
    grads = [
        lax.dynamic_update_index_in_dim(x, t, 1 - mine, 0)
        for x, t in zip(mine_gud, (take_g, take_u, take_d))
    ]
    return out, norm, grad_routes, *grads


def solution(mesh):
    tokens = P(("dp", "tensor"), None)
    weights = P("dp", "tensor", None)
    return jax.shard_map(
        body,
        mesh=mesh,
        in_specs=(tokens, tokens, P(), tokens, tokens, weights, weights, weights),
        out_specs=(tokens, P(), tokens, weights, weights, weights),
        check_vma=False,
    )
```

```python
import functools

import jax
import jax.numpy as jnp
import numpy as np
from jax import lax
from jax.experimental import pallas as pl
from jax.experimental.pallas import tpu as pltpu
from jax.sharding import PartitionSpec as P

EPS = 1e-06
TOK = 128
D = 4096
HALF = D // 2
QUART = D // 4
CAP = 6
N_DP = 16
SLICE = 192
ROWS = N_DP * CAP
PART = 4 * ROWS
EXTRA = 128
VMEM = 56 * 1024 * 1024
F_STEP, W_STEP = 2048, 2048
F32 = jnp.float32
BF16 = jnp.bfloat16


def params():
    return pltpu.CompilerParams(vmem_limit_bytes=VMEM)


def whole(shape):
    return pl.BlockSpec(shape, lambda *_: (0,) * len(shape))


def dot(a, b):
    return jnp.dot(a, b, preferred_element_type=F32)


def dot_nt(a, b):
    return lax.dot_general(a, b, (((1,), (1,)), ((), ())), preferred_element_type=F32)


def iota(shape, dim):
    return lax.broadcasted_iota(jnp.int32, shape, dim)


def stack(refs, cols=slice(None)):
    return jnp.concatenate([r[:, cols] for r in refs], axis=0)


def move(i, kind):
    z, y = divmod(i % 8, 4)
    if kind == "z":
        z = z ^ 1
    elif (kind == "trade") == (i // 8 % 2 == 0):
        y = y ^ 1
    else:
        y = 3 - y
    return i // 8 * 8 + z * 4 + y


AXES = ("dp", "tensor")
PERMS = {k: [(i, move(i, k)) for i in range(128)] for k in ("trade", "y", "z")}


def trade(x):
    return lax.ppermute(x, AXES, PERMS["trade"])


def trade_for(core, x):
    return lax.ppermute(x, "tensor", [(t, move(core * 8 + t, "trade") % 8) for t in range(8)])


def over_y(x):
    return lax.ppermute(x, AXES, PERMS["y"])


def over_z(x):
    return lax.ppermute(x, AXES, PERMS["z"])


def owned():
    y = lax.axis_index("tensor") & 3
    return jnp.where((y == 0) | (y == 3), 1, 0).astype(jnp.int32), y >> 1


def tree_barrier(tree):
    leaves, shape = jax.tree.flatten(tree)
    return jax.tree.unflatten(shape, barrier(*leaves))


def column(row):
    diagonal = iota((TOK, TOK), 0) == iota((TOK, TOK), 1)
    return jnp.sum(jnp.where(diagonal, row, jnp.zeros_like(row)), axis=1, keepdims=True)


def rank_of(rrow, axis):
    same = column(rrow) == rrow
    earlier = iota((TOK, TOK), axis) < iota((TOK, TOK), 1 - axis)
    return jnp.sum(jnp.where(same & earlier, 1, 0), axis=axis, keepdims=True)


def place_of(expert, own_ref):
    dp = expert >> 1
    mine = jnp.where((dp & 1) == 0, own_ref[0], own_ref[1])
    return dp, (expert & 1) ^ mine


def dispatch_kernel(turn, own_ref, h_ref, c_ref, gain_ref, rrow_ref, wrow_ref, *outs):
    rows = 4 * ROWS
    len_out = rows // len(outs)
    x = h_ref[...].astype(F32)
    scale = lax.rsqrt(jnp.mean(x * x, axis=-1, keepdims=True) + EPS)
    weight = column(wrow_ref[...].astype(F32))
    rank = rank_of(rrow_ref[...], 0)
    dp, when = place_of(rrow_ref[...], own_ref)
    if len(outs) == 2:
        dp = (dp >> 1) + (dp & 1) * (N_DP // 2)
    slot = jnp.where(when == turn, dp * (4 * CAP) + rank, -4 * CAP)
    at = iota((rows, TOK), 0)
    pick = [jnp.where(at == slot + k * CAP, 1.0, 0.0).astype(BF16) for k in range(4)]
    pick = jnp.concatenate(pick, axis=1)
    wide = 512
    for j in range(HALF // wide):
        value = []
        for half in range(2):
            cols = slice(half * HALF + j * wide, half * HALF + (j + 1) * wide)
            value.append((x[:, cols] * scale * gain_ref[:, cols]).astype(BF16))
            value.append((c_ref[:, cols].astype(F32) * weight).astype(BF16))
        rows_j = dot(pick, jnp.concatenate(value, axis=0)).astype(BF16)
        for k, out in enumerate(outs):
            out[:, j * wide : (j + 1) * wide] = rows_j[k * len_out : (k + 1) * len_out]


def dispatch(turn, own, h, c, gain, rrow, wrow):
    return pl.pallas_call(
        functools.partial(dispatch_kernel, turn),
        in_specs=[pl.BlockSpec(memory_space=pltpu.SMEM)] + [pl.BlockSpec(memory_space=pltpu.VMEM)] * 5,
        out_shape=[jax.ShapeDtypeStruct((4 * ROWS // (1 + turn), HALF), BF16)] * (1 + turn),
        compiler_params=params(),
        cost_estimate=pl.CostEstimate(flops=2 * 384 * 512 * HALF, bytes_accessed=4 << 20, transcendentals=0),
        name="dispatch",
    )(own, h, c, gain, rrow, wrow)


def sort_matrix():
    out = np.zeros((4 * ROWS, 4 * ROWS), np.float32)
    for block in range(4):
        for src in range(N_DP):
            for k in range(CAP):
                out[block * ROWS + src * CAP + k, src * 4 * CAP + block * CAP + k] = 1.0
    return out


def sort_kernel(m_ref, x_ref, *outs):
    n = 2 * ROWS // len(outs)
    for half in range(2):
        for k, out in enumerate(outs):
            lo = half * 2 * ROWS + k * n
            out[:, half * HALF : (half + 1) * HALF] = dot(m_ref[lo : lo + n, :], x_ref[...]).astype(BF16)


def sort_rows(x, parts):
    return pl.pallas_call(
        sort_kernel,
        out_shape=[jax.ShapeDtypeStruct((2 * ROWS // parts, D), BF16)] * parts,
        compiler_params=params(),
        cost_estimate=pl.CostEstimate(flops=2 * 384 * 384 * HALF, bytes_accessed=4 << 20, transcendentals=0),
        name="sort_rows",
    )(jnp.asarray(sort_matrix(), BF16), x)


def tie(x, *others):
    return barrier(x, *others)[0]


def barrier(*arrays):
    return list(lax.optimization_barrier(arrays))


def pieces(hs, cs, wide):
    specs = [pl.BlockSpec((ROWS, wide), lambda s, own, k=k: (k, s)) for _, k in hs + cs]
    return specs, [x for x, _ in hs + cs]


def slices(count, wide):
    return [pl.BlockSpec((SLICE, wide), lambda s, own, k=k: (k, s)) for k in range(count)]


def add(a, b):
    return (a.astype(F32) + b.astype(F32)).astype(BF16)


def sum_dp(x, bit):
    return x + lax.ppermute(x, "dp", [(i, i ^ bit) for i in range(16)])


def spread(x):
    return jnp.where(iota((8, D), 0) == lax.axis_index("tensor"), x, 0.0)


def reduce_first(left, right):
    return (over_z(left[3]), over_z(left[2])), (over_y(right[3]), over_y(right[1]))


def reduce_second(left, right, got_l, got_r):
    sum_l = left[0], got_l[1], over_y(add(left[1], got_l[0]))
    sum_r = right[0], got_r[1], over_z(add(right[2], got_r[0]))
    return sum_l, sum_r


def forward_kernel(own_ref, *refs):
    hs, cs = refs[:4], refs[4:8]
    gate_ref, up_ref, down_ref, gate2_ref, up2_ref, down2_ref = refs[8:14]
    dgu_ref, dgu_t_ref, act_t_ref, pw_ref = refs[14:18]
    acc_g, acc_u, acc_b = refs[18:]
    s = pl.program_id(0)
    h, c = stack(hs), stack(cs)
    g = dot_nt(h, jnp.concatenate([gate_ref[0], gate2_ref[...]], axis=0))
    u = dot_nt(h, jnp.concatenate([up_ref[0], up2_ref[...]], axis=0))
    b = dot_nt(c, jnp.concatenate([down_ref[0], down2_ref[...]], axis=0))

    @pl.when(s == 0)
    def _():
        acc_g[...] = g
        acc_u[...] = u
        acc_b[...] = b

    @pl.when(s > 0)
    def _():
        acc_g[...] += g
        acc_u[...] += u
        acc_b[...] += b

    @pl.when(s == pl.num_programs(0) - 1)
    def _():
        gate, upp, back = acc_g[...], acc_u[...], acc_b[...]
        sig = jax.nn.sigmoid(gate)
        silu = gate * sig
        act = silu * upp
        dgate = back * upp * sig * (1.0 + gate * (1.0 - sig))
        dup = back * silu
        for part in range(2):
            cols = slice(part * SLICE, (part + 1) * SLICE)
            lo = part * 2 * SLICE
            dgu_ref[:, lo : lo + SLICE] = dgate[:, cols].astype(BF16)
            dgu_ref[:, lo + SLICE : lo + 2 * SLICE] = dup[:, cols].astype(BF16)
        dgate_t, dup_t = dgate.T.astype(BF16), dup.T.astype(BF16)
        for part in range(2):
            rows = slice(part * SLICE, (part + 1) * SLICE)
            lo = part * 2 * SLICE
            dgu_t_ref[lo : lo + SLICE, :] = dgate_t[rows]
            dgu_t_ref[lo + SLICE : lo + 2 * SLICE, :] = dup_t[rows]
        act_t_ref[...] = act.T.astype(BF16)
        pw = jnp.sum(act * back, axis=-1, keepdims=True)
        high = pw.astype(BF16).astype(F32)
        lane = iota((PART, EXTRA), 1)
        value = jnp.where(lane == 0, high, jnp.where(lane == 1, pw - high, 0.0))
        pw_ref[...] = value.astype(BF16)


def forward(own, hs, cs, weights, got):
    step = F_STEP
    specs, arrays = pieces(hs, cs, step)
    mine = pl.BlockSpec((1, SLICE, step), lambda s, own: (own[0], 0, s))
    shapes = [(PART, 4 * SLICE), (4 * SLICE, PART), (2 * SLICE, PART), (PART, EXTRA)]
    return pl.pallas_call(
        forward_kernel,
        grid_spec=pltpu.PrefetchScalarGridSpec(
            num_scalar_prefetch=1,
            grid=(D // step,),
            in_specs=specs + [mine] * 3 + slices(1, step) * 3,
            out_specs=[whole(s) for s in shapes],
            scratch_shapes=[pltpu.VMEM((PART, 2 * SLICE), F32)] * 3,
        ),
        out_shape=[jax.ShapeDtypeStruct(s, BF16) for s in shapes],
        compiler_params=params(),
        cost_estimate=pl.CostEstimate(
            flops=2 * PART * 6 * SLICE * D, bytes_accessed=16 << 20, transcendentals=PART * 384
        ),
        name="expert_forward",
    )(own, *arrays, *weights, *got)


def rows_kernel(own_ref, dgu_ref, pw_ref, *refs):
    hs = refs[:4]
    gate_ref, up_ref, gate2_ref, up2_ref = refs[4:8]
    left, right, norm_ref = refs[8:12], refs[12:16], refs[16]
    s = pl.program_id(0)
    w = jnp.concatenate([gate_ref[0], up_ref[0], gate2_ref[...], up2_ref[...]], axis=0)
    value = dot(dgu_ref[...], w)
    norm_ref[...] = jnp.sum(value * stack(hs).astype(F32), axis=0, keepdims=True)
    value = value.astype(BF16)

    @pl.when(s == 0)
    def _():
        for k, out in enumerate(left):
            out[...] = value[k * ROWS : (k + 1) * ROWS]

    @pl.when(s == 1)
    def _():
        for k, out in enumerate(right):
            out[:, :HALF] = value[k * ROWS : (k + 1) * ROWS]
            out[:, HALF:] = pw_ref[k * ROWS : (k + 1) * ROWS, :]


def expert_rows(own, dgu, pw, hs, weights, got):
    wide = HALF
    mine = pl.BlockSpec((1, SLICE, wide), lambda s, own: (own[0], 0, s))
    specs, arrays = pieces(hs, [], wide)
    shapes = [(ROWS, HALF)] * 4 + [(ROWS, HALF + EXTRA)] * 4
    *out, norm = pl.pallas_call(
        rows_kernel,
        grid_spec=pltpu.PrefetchScalarGridSpec(
            num_scalar_prefetch=1,
            grid=(D // wide,),
            in_specs=[whole((PART, 4 * SLICE)), whole((PART, EXTRA))] + specs + [mine, mine] + slices(1, wide) * 2,
            out_specs=[whole(x) for x in shapes] + [pl.BlockSpec((1, wide), lambda s, own: (0, s))],
        ),
        out_shape=[jax.ShapeDtypeStruct(x, BF16) for x in shapes] + [jax.ShapeDtypeStruct((1, D), F32)],
        compiler_params=params(),
        cost_estimate=pl.CostEstimate(
            flops=2 * PART * 4 * SLICE * D, bytes_accessed=10 << 20, transcendentals=0
        ),
        name="expert_rows",
    )(own, dgu, pw, *arrays, weights[0], weights[1], got[0], got[1])
    return out[:4], out[4:], norm


def weights_kernel(part, kinds, own_ref, *refs):
    outs = refs[-len(kinds) :]
    hs, cs = refs[:8], refs[8:16]
    if 2 not in kinds:
        lhs, lo, hi, rows = refs[8:10], part * 2 + kinds[0], part * 2 + kinds[-1] + 1, hs
        values = dot(jnp.concatenate([r[lo * SLICE : hi * SLICE] for r in lhs], axis=1), stack(rows))
        values = [values[k * SLICE : (k + 1) * SLICE] for k in range(len(kinds))]
    elif kinds == (2,):
        lhs, rows = refs[8:10], hs
        values = [dot(jnp.concatenate([r[part * SLICE : (part + 1) * SLICE] for r in lhs], axis=1), stack(rows))]
    else:
        lo = part * 2 * SLICE
        lhs = [r[lo : lo + 2 * SLICE] for r in refs[16:18]]
        values = dot(jnp.concatenate(lhs, axis=1), stack(hs))
        values = [values[:SLICE], values[SLICE:]]
        lhs = [r[part * SLICE : (part + 1) * SLICE] for r in refs[18:20]]
        values.append(dot(jnp.concatenate(lhs, axis=1), stack(cs)))
    for out, value in zip(outs, values):
        if part == 0:
            out[0] = value.astype(BF16)
        else:
            out[...] = value.astype(BF16)


def expert_weights(part, kinds, own, hs, cs, dgu_t, act_t, after):
    wide = W_STEP
    hs, dgu_t = (hs, dgu_t) if 0 in kinds or 1 in kinds else ([], ())
    cs, act_t = (cs, act_t) if 2 in kinds else ([], ())
    specs, arrays = pieces(hs, cs, wide)
    if part == 0:
        made = pl.BlockSpec((1, SLICE, wide), lambda j, own: (own[0], 0, j))
        grad = jax.ShapeDtypeStruct((2, SLICE, D), BF16)
    else:
        made = pl.BlockSpec((SLICE, wide), lambda j, own: (0, j))
        grad = jax.ShapeDtypeStruct((SLICE, D), BF16)
    out = pl.pallas_call(
        functools.partial(weights_kernel, part, kinds),
        grid_spec=pltpu.PrefetchScalarGridSpec(
            num_scalar_prefetch=1,
            grid=(D // wide,),
            in_specs=specs
            + [whole((4 * SLICE, PART))] * len(dgu_t)
            + [whole((2 * SLICE, PART))] * len(act_t)
            + [pl.BlockSpec(memory_space=pl.ANY)] * len(after),
            out_specs=[made] * len(kinds),
        ),
        out_shape=[grad] * len(kinds),
        compiler_params=params(),
        cost_estimate=pl.CostEstimate(
            flops=2 * 2 * PART * len(kinds) * SLICE * D, bytes_accessed=len(kinds) * 6 << 20, transcendentals=0
        ),
        name="expert_weights",
    )(own, *arrays, *dgu_t, *act_t, *after)
    return list(out)


def pack_matrix():
    out = np.zeros((4 * ROWS, 4 * ROWS), np.float32)
    for quarter in range(4):
        for src in range(N_DP):
            for k in range(CAP):
                out[src * 4 * CAP + quarter * CAP + k, quarter * ROWS + src * CAP + k] = 1.0
    return out


def pack_kernel(m_ref, *refs):
    left, right, out_ref = refs[:3], refs[3:6], refs[6]

    def total(refs, cols):
        p, q, r = [x[:, cols].astype(F32) for x in refs]
        return p + q + r

    wide = 512
    for j in range(QUART // wide):
        lo = j * wide
        rows = [total(x, slice(at, at + wide)).astype(BF16) for x in (left, right) for at in (lo, lo + QUART)]
        out_ref[:, lo : lo + wide] = dot(m_ref[...], jnp.concatenate(rows, axis=0)).astype(BF16)
    pw = total(right, slice(HALF, HALF + EXTRA))
    pw = pw[:, 0:1] + pw[:, 1:2]
    high = pw.astype(BF16).astype(F32)
    lane = iota((ROWS, EXTRA), 1)
    value = jnp.where(lane == 0, high, jnp.where(lane == 1, pw - high, 0.0)).astype(BF16)
    out_ref[:, QUART:] = dot(m_ref[:, :ROWS], value).astype(BF16)


def pack(left, right):
    return pl.pallas_call(
        pack_kernel,
        out_shape=jax.ShapeDtypeStruct((4 * ROWS, QUART + EXTRA), BF16),
        compiler_params=params(),
        cost_estimate=pl.CostEstimate(flops=2 * 384 * 384 * QUART, bytes_accessed=4 << 20, transcendentals=0),
        name="pack_rows",
    )(jnp.asarray(pack_matrix(), BF16), *left, *right)


def combine_kernel(own_ref, r0_ref, r1_ref, h_ref, c_ref, gain_ref, rrow_ref, wrow_ref, out_ref, routes_ref):
    rank = rank_of(rrow_ref[...], 1)
    dp, when = place_of(column(rrow_ref[...]), own_ref)
    place = dp * (4 * CAP) + rank + when * (4 * ROWS)
    at = iota((TOK, 8 * ROWS), 1)
    r = jnp.concatenate([r0_ref[...], r1_ref[...]], axis=0)
    picks = [jnp.where(at == place + q * CAP, 1.0, 0.0).astype(BF16) for q in range(4)]
    pw = dot(picks[0], r[:, QUART:])
    diagonal = iota((TOK, TOK), 0) == iota((TOK, TOK), 1)
    pw = jnp.sum(jnp.where(diagonal, pw[:, 0:1] + pw[:, 1:2], 0.0), axis=0, keepdims=True)
    routes_ref[...] = pw / wrow_ref[...].astype(F32)
    g = jnp.concatenate([dot(p, r[:, :QUART]) for p in picks], axis=1)
    x = h_ref[...].astype(F32)
    scale = lax.rsqrt(jnp.mean(x * x, axis=-1, keepdims=True) + EPS)
    x = x * scale
    dx = g * gain_ref[...]
    mix = jnp.mean(dx * x, axis=-1, keepdims=True)
    out_ref[...] = (c_ref[...].astype(F32) + scale * (dx - x * mix)).astype(BF16)


def combine(own, r0, r1, h, c, gain, rrow, wrow):
    return pl.pallas_call(
        combine_kernel,
        in_specs=[pl.BlockSpec(memory_space=pltpu.SMEM)] + [pl.BlockSpec(memory_space=pltpu.VMEM)] * 7,
        out_shape=[
            jax.ShapeDtypeStruct((TOK, D), BF16),
            jax.ShapeDtypeStruct((1, TOK), F32),
        ],
        compiler_params=params(),
        cost_estimate=pl.CostEstimate(flops=2 * 128 * 768 * D, bytes_accessed=5 << 20, transcendentals=0),
        name="combine",
    )(own, r0, r1, h, c, gain, rrow, wrow)


def exchange(x):
    shaped = x.reshape((N_DP, -1) + x.shape[1:])
    got = lax.all_to_all(shaped, "dp", split_axis=0, concat_axis=0, tiled=True)
    return got.reshape(x.shape)


def body(h, c, gain, routes, w, w_gate, w_up, w_down):
    gain = gain.reshape(1, D)
    rrow, wrow = routes.reshape(1, TOK), w.reshape(1, TOK)
    own0, own1 = owned()
    owns = jnp.stack([own0, own1])
    mine = jnp.where((lax.axis_index("dp") & 1) == 0, own0, own1)
    own = mine.reshape(1)
    weights = (w_gate, w_up, w_down)

    slots_a = dispatch(1, owns, h, c, gain, rrow, wrow)
    (slots_b,) = dispatch(0, owns, tie(h, *slots_a), c, gain, rrow, wrow)
    slots_a = [trade_for(core, x).reshape(N_DP // 2, -1, HALF) for core, x in enumerate(slots_a)]
    got_b = exchange(slots_b)
    leave = [lax.dynamic_index_in_dim(x, 1 - mine, 0, keepdims=False) for x in weights]
    got_g = trade(leave[0])
    got_b, got_g, *slots_a, leave_u, leave_d = barrier(got_b, got_g, *slots_a, *leave[1:])
    got_u = trade(leave_u)
    bh, bc = sort_rows(got_b, 2)
    got_a = exchange(jnp.stack(slots_a, axis=1).reshape(4 * ROWS, HALF))
    got_a, got_u, bh, bc = barrier(got_a, got_u, bh, bc)
    got_d = trade(leave_d)
    (a,) = sort_rows(got_a, 1)
    az, ay = over_z(a), over_y(a)
    az, ay, bh, bc, got_d = barrier(az, ay, bh, bc, got_d)
    got = got_g, got_u, got_d
    ao, bzh, bzc, byh, byc = over_y(az), over_z(bh), over_z(bc), over_y(bh), over_y(bc)
    piece_a = (a, ay, az, ao)
    hs_a, cs_a = [(x, 0) for x in piece_a], [(x, 1) for x in piece_a]
    dgu_a, dgu_ta, act_ta, pw_a = forward(own, hs_a, cs_a, weights, got)
    bzh, bzc, byh, byc, dgu_a = barrier(bzh, bzc, byh, byc, dgu_a)
    boh, boc = over_y(bzh), over_y(bzc)
    la, ra, norm_a = expert_rows(own, dgu_a, pw_a, hs_a, weights, got)
    al, ar = reduce_first(la, ra)

    hs_b, cs_b = [(x, 0) for x in (bh, byh, bzh, boh)], [(x, 0) for x in (bc, byc, bzc, boc)]
    dgu_b, dgu_tb, act_tb, pw_b = forward(own, hs_b, cs_b, weights, got)
    dgu_b, *al, = barrier(dgu_b, *al)
    dgu_b, *ar, = barrier(dgu_b, *ar)
    al, ar = reduce_second(la, ra, al, ar)
    lb, rb, norm_b = expert_rows(own, dgu_b, pw_b, hs_b, weights, got)
    norm = (norm_a + norm_b) / gain
    hs, cs, dgu_t, act_t = hs_a + hs_b, cs_a + cs_b, (dgu_ta, dgu_tb), (act_ta, act_tb)
    grads = functools.partial(expert_weights, own=own, hs=hs, cs=cs, dgu_t=dgu_t, act_t=act_t)
    lb, rb, al, ar, norm = tree_barrier((lb, rb, al, ar, norm))
    bl, br = reduce_first(lb, rb)
    packed_a = pack(al, ar)
    norm, sent_a = barrier(sum_dp(norm, 1), packed_a)
    packed_a = trade(packed_a)
    (give_g,) = grads(1, (0,), after=(lb[0], sent_a, norm))
    norm, give_g = barrier(sum_dp(norm, 4), give_g)
    take_g = trade(give_g)
    (give_u,) = grads(1, (1,), after=(give_g, norm))
    norm, packed_a, give_u, *far = barrier(sum_dp(norm, 8), packed_a, give_u, *bl, *br)
    sum_l, sum_r = add(lb[1], far[0]), add(rb[2], far[2])
    sum_l, sum_r, packed_a, norm, give_u = barrier(sum_l, sum_r, packed_a, norm, give_u)
    bl, br = (lb[0], far[1], over_y(sum_l)), (rb[0], far[3], over_z(sum_r))
    take_u = trade(give_u)
    r_a = exchange(packed_a)
    mine_gud = grads(0, (0, 1, 2), after=(sum_l, sum_r))
    norm, mine_gud[0] = barrier(spread(sum_dp(norm, 2)), mine_gud[0])
    (give_d,) = grads(1, (2,), after=(mine_gud[0], norm))
    norm, give_d = barrier(norm + over_z(norm), give_d)
    norm = norm + over_y(norm)
    norm, *far = barrier(norm, *bl, *br)
    norm = norm + trade(norm)
    packed_b, r_a, take_g = barrier(pack(far[:3], far[3:]), r_a, take_g)
    r_b = exchange(packed_b)
    take_d = trade(give_d)
    r_b, take_u = barrier(r_b, take_u)
    norm = jnp.sum(norm, axis=0)
    out, grad_routes = combine(owns, r_b, r_a, h, c, gain, rrow, wrow)
    grad_routes = grad_routes.reshape(TOK, 1)
    grads = [
        lax.dynamic_update_index_in_dim(x, t, 1 - mine, 0)
        for x, t in zip(mine_gud, (take_g, take_u, take_d))
    ]
    return out, norm, grad_routes, *grads


def solution(mesh):
    tokens = P(("dp", "tensor"), None)
    weights = P("dp", "tensor", None)
    return jax.shard_map(
        body,
        mesh=mesh,
        in_specs=(tokens, tokens, P(), tokens, tokens, weights, weights, weights),
        out_specs=(tokens, P(), tokens, weights, weights, weights),
        check_vma=False,
    )
```

```python
import functools

import jax
import jax.numpy as jnp
import numpy as np
from jax import lax
from jax.experimental import pallas as pl
from jax.experimental.pallas import tpu as pltpu
from jax.sharding import PartitionSpec as P

EPS = 1e-06
TOK = 128
D = 4096
HALF = D // 2
QUART = D // 4
CAP = 6
N_DP = 16
SLICE = 192
ROWS = N_DP * CAP
PART = 4 * ROWS
EXTRA = 128
VMEM = 56 * 1024 * 1024
F_STEP, W_STEP = 2048, 2048
F32 = jnp.float32
BF16 = jnp.bfloat16


def params():
    return pltpu.CompilerParams(vmem_limit_bytes=VMEM)


def whole(shape):
    return pl.BlockSpec(shape, lambda *_: (0,) * len(shape))


def dot(a, b):
    return jnp.dot(a, b, preferred_element_type=F32)


def dot_nt(a, b):
    return lax.dot_general(a, b, (((1,), (1,)), ((), ())), preferred_element_type=F32)


def iota(shape, dim):
    return lax.broadcasted_iota(jnp.int32, shape, dim)


def stack(refs, cols=slice(None)):
    return jnp.concatenate([r[:, cols] for r in refs], axis=0)


def move(i, kind):
    z, y = divmod(i % 8, 4)
    if kind == "z":
        z = z ^ 1
    elif (kind == "trade") == (i // 8 % 2 == 0):
        y = y ^ 1
    else:
        y = 3 - y
    return i // 8 * 8 + z * 4 + y


AXES = ("dp", "tensor")
PERMS = {k: [(i, move(i, k)) for i in range(128)] for k in ("trade", "y", "z")}


def trade(x):
    return lax.ppermute(x, AXES, PERMS["trade"])


def trade_for(core, x):
    return lax.ppermute(x, "tensor", [(t, move(core * 8 + t, "trade") % 8) for t in range(8)])


def over_y(x):
    return lax.ppermute(x, AXES, PERMS["y"])


def over_z(x):
    return lax.ppermute(x, AXES, PERMS["z"])


def owned():
    y = lax.axis_index("tensor") & 3
    return jnp.where((y == 0) | (y == 3), 1, 0).astype(jnp.int32), y >> 1


def tree_barrier(tree):
    leaves, shape = jax.tree.flatten(tree)
    return jax.tree.unflatten(shape, barrier(*leaves))


def column(row):
    diagonal = iota((TOK, TOK), 0) == iota((TOK, TOK), 1)
    return jnp.sum(jnp.where(diagonal, row, jnp.zeros_like(row)), axis=1, keepdims=True)


def rank_of(rrow, axis):
    same = column(rrow) == rrow
    earlier = iota((TOK, TOK), axis) < iota((TOK, TOK), 1 - axis)
    return jnp.sum(jnp.where(same & earlier, 1, 0), axis=axis, keepdims=True)


def place_of(expert, own_ref):
    dp = expert >> 1
    mine = jnp.where((dp & 1) == 0, own_ref[0], own_ref[1])
    return dp, (expert & 1) ^ mine


def dispatch_kernel(turn, own_ref, h_ref, c_ref, gain_ref, rrow_ref, wrow_ref, *outs):
    rows = 4 * ROWS
    len_out = rows // len(outs)
    x = h_ref[...].astype(F32)
    scale = lax.rsqrt(jnp.mean(x * x, axis=-1, keepdims=True) + EPS)
    weight = column(wrow_ref[...].astype(F32))
    rank = rank_of(rrow_ref[...], 0)
    dp, when = place_of(rrow_ref[...], own_ref)
    if len(outs) == 2:
        dp = (dp >> 1) + (dp & 1) * (N_DP // 2)
    slot = jnp.where(when == turn, dp * (4 * CAP) + rank, -4 * CAP)
    at = iota((rows, TOK), 0)
    pick = [jnp.where(at == slot + k * CAP, 1.0, 0.0).astype(BF16) for k in range(4)]
    pick = jnp.concatenate(pick, axis=1)
    wide = 512
    for j in range(HALF // wide):
        value = []
        for half in range(2):
            cols = slice(half * HALF + j * wide, half * HALF + (j + 1) * wide)
            value.append((x[:, cols] * scale * gain_ref[:, cols]).astype(BF16))
            value.append((c_ref[:, cols].astype(F32) * weight).astype(BF16))
        rows_j = dot(pick, jnp.concatenate(value, axis=0)).astype(BF16)
        for k, out in enumerate(outs):
            out[:, j * wide : (j + 1) * wide] = rows_j[k * len_out : (k + 1) * len_out]


def dispatch(turn, own, h, c, gain, rrow, wrow):
    return pl.pallas_call(
        functools.partial(dispatch_kernel, turn),
        in_specs=[pl.BlockSpec(memory_space=pltpu.SMEM)] + [pl.BlockSpec(memory_space=pltpu.VMEM)] * 5,
        out_shape=[jax.ShapeDtypeStruct((4 * ROWS // (1 + turn), HALF), BF16)] * (1 + turn),
        compiler_params=params(),
        cost_estimate=pl.CostEstimate(flops=2 * 384 * 512 * HALF, bytes_accessed=4 << 20, transcendentals=0),
        name="dispatch",
    )(own, h, c, gain, rrow, wrow)


def sort_matrix():
    out = np.zeros((4 * ROWS, 4 * ROWS), np.float32)
    for block in range(4):
        for src in range(N_DP):
            for k in range(CAP):
                out[block * ROWS + src * CAP + k, src * 4 * CAP + block * CAP + k] = 1.0
    return out


def sort_kernel(m_ref, x_ref, *outs):
    n = 2 * ROWS // len(outs)
    for half in range(2):
        for k, out in enumerate(outs):
            lo = half * 2 * ROWS + k * n
            out[:, half * HALF : (half + 1) * HALF] = dot(m_ref[lo : lo + n, :], x_ref[...]).astype(BF16)


def sort_rows(x, parts):
    return pl.pallas_call(
        sort_kernel,
        out_shape=[jax.ShapeDtypeStruct((2 * ROWS // parts, D), BF16)] * parts,
        compiler_params=params(),
        cost_estimate=pl.CostEstimate(flops=2 * 384 * 384 * HALF, bytes_accessed=4 << 20, transcendentals=0),
        name="sort_rows",
    )(jnp.asarray(sort_matrix(), BF16), x)


def tie(x, *others):
    return barrier(x, *others)[0]


def barrier(*arrays):
    return list(lax.optimization_barrier(arrays))


def pieces(hs, cs, wide):
    specs = [pl.BlockSpec((ROWS, wide), lambda s, own, k=k: (k, s)) for _, k in hs + cs]
    return specs, [x for x, _ in hs + cs]


def slices(count, wide):
    return [pl.BlockSpec((SLICE, wide), lambda s, own, k=k: (k, s)) for k in range(count)]


def add(a, b):
    return (a.astype(F32) + b.astype(F32)).astype(BF16)


def sum_dp(x, bit):
    return x + lax.ppermute(x, "dp", [(i, i ^ bit) for i in range(16)])


def spread(x):
    return jnp.where(iota((8, D), 0) == lax.axis_index("tensor"), x, 0.0)


def reduce_first(left, right):
    return (over_z(left[3]), over_z(left[2])), (over_y(right[3]), over_y(right[1]))


def reduce_second(left, right, got_l, got_r):
    sum_l = left[0], got_l[1], over_y(add(left[1], got_l[0]))
    sum_r = right[0], got_r[1], over_z(add(right[2], got_r[0]))
    return sum_l, sum_r


def forward_kernel(own_ref, *refs):
    hs, cs = refs[:4], refs[4:8]
    gate_ref, up_ref, down_ref, gate2_ref, up2_ref, down2_ref = refs[8:14]
    dgu_ref, dgu_t_ref, act_t_ref, pw_ref = refs[14:18]
    acc_g, acc_u, acc_b = refs[18:]
    s = pl.program_id(0)
    h, c = stack(hs), stack(cs)
    g = dot_nt(h, jnp.concatenate([gate_ref[0], gate2_ref[...]], axis=0))
    u = dot_nt(h, jnp.concatenate([up_ref[0], up2_ref[...]], axis=0))
    b = dot_nt(c, jnp.concatenate([down_ref[0], down2_ref[...]], axis=0))

    @pl.when(s == 0)
    def _():
        acc_g[...] = g
        acc_u[...] = u
        acc_b[...] = b

    @pl.when(s > 0)
    def _():
        acc_g[...] += g
        acc_u[...] += u
        acc_b[...] += b

    @pl.when(s == pl.num_programs(0) - 1)
    def _():
        gate, upp, back = acc_g[...], acc_u[...], acc_b[...]
        sig = jax.nn.sigmoid(gate)
        silu = gate * sig
        act = silu * upp
        dgate = back * upp * sig * (1.0 + gate * (1.0 - sig))
        dup = back * silu
        for part in range(2):
            cols = slice(part * SLICE, (part + 1) * SLICE)
            lo = part * 2 * SLICE
            dgu_ref[:, lo : lo + SLICE] = dgate[:, cols].astype(BF16)
            dgu_ref[:, lo + SLICE : lo + 2 * SLICE] = dup[:, cols].astype(BF16)
        dgate_t, dup_t = dgate.T.astype(BF16), dup.T.astype(BF16)
        for part in range(2):
            rows = slice(part * SLICE, (part + 1) * SLICE)
            lo = part * 2 * SLICE
            dgu_t_ref[lo : lo + SLICE, :] = dgate_t[rows]
            dgu_t_ref[lo + SLICE : lo + 2 * SLICE, :] = dup_t[rows]
        act_t_ref[...] = act.T.astype(BF16)
        pw = jnp.sum(act * back, axis=-1, keepdims=True)
        high = pw.astype(BF16).astype(F32)
        lane = iota((PART, EXTRA), 1)
        value = jnp.where(lane == 0, high, jnp.where(lane == 1, pw - high, 0.0))
        pw_ref[...] = value.astype(BF16)


def forward(own, hs, cs, weights, got):
    step = F_STEP
    specs, arrays = pieces(hs, cs, step)
    mine = pl.BlockSpec((1, SLICE, step), lambda s, own: (own[0], 0, s))
    shapes = [(PART, 4 * SLICE), (4 * SLICE, PART), (2 * SLICE, PART), (PART, EXTRA)]
    return pl.pallas_call(
        forward_kernel,
        grid_spec=pltpu.PrefetchScalarGridSpec(
            num_scalar_prefetch=1,
            grid=(D // step,),
            in_specs=specs + [mine] * 3 + slices(1, step) * 3,
            out_specs=[whole(s) for s in shapes],
            scratch_shapes=[pltpu.VMEM((PART, 2 * SLICE), F32)] * 3,
        ),
        out_shape=[jax.ShapeDtypeStruct(s, BF16) for s in shapes],
        compiler_params=params(),
        cost_estimate=pl.CostEstimate(
            flops=2 * PART * 6 * SLICE * D, bytes_accessed=16 << 20, transcendentals=PART * 384
        ),
        name="expert_forward",
    )(own, *arrays, *weights, *got)


def rows_kernel(own_ref, dgu_ref, pw_ref, *refs):
    hs = refs[:4]
    gate_ref, up_ref, gate2_ref, up2_ref = refs[4:8]
    left, right, norm_ref = refs[8:12], refs[12:16], refs[16]
    s = pl.program_id(0)
    w = jnp.concatenate([gate_ref[0], up_ref[0], gate2_ref[...], up2_ref[...]], axis=0)
    value = dot(dgu_ref[...], w)
    norm_ref[...] = jnp.sum(value * stack(hs).astype(F32), axis=0, keepdims=True)
    value = value.astype(BF16)

    @pl.when(s == 0)
    def _():
        for k, out in enumerate(left):
            out[...] = value[k * ROWS : (k + 1) * ROWS]

    @pl.when(s == 1)
    def _():
        for k, out in enumerate(right):
            out[:, :HALF] = value[k * ROWS : (k + 1) * ROWS]
            out[:, HALF:] = pw_ref[k * ROWS : (k + 1) * ROWS, :]


def expert_rows(own, dgu, pw, hs, weights, got):
    wide = HALF
    mine = pl.BlockSpec((1, SLICE, wide), lambda s, own: (own[0], 0, s))
    specs, arrays = pieces(hs, [], wide)
    shapes = [(ROWS, HALF)] * 4 + [(ROWS, HALF + EXTRA)] * 4
    *out, norm = pl.pallas_call(
        rows_kernel,
        grid_spec=pltpu.PrefetchScalarGridSpec(
            num_scalar_prefetch=1,
            grid=(D // wide,),
            in_specs=[whole((PART, 4 * SLICE)), whole((PART, EXTRA))] + specs + [mine, mine] + slices(1, wide) * 2,
            out_specs=[whole(x) for x in shapes] + [pl.BlockSpec((1, wide), lambda s, own: (0, s))],
        ),
        out_shape=[jax.ShapeDtypeStruct(x, BF16) for x in shapes] + [jax.ShapeDtypeStruct((1, D), F32)],
        compiler_params=params(),
        cost_estimate=pl.CostEstimate(
            flops=2 * PART * 4 * SLICE * D, bytes_accessed=10 << 20, transcendentals=0
        ),
        name="expert_rows",
    )(own, dgu, pw, *arrays, weights[0], weights[1], got[0], got[1])
    return out[:4], out[4:], norm


def weights_kernel(part, kinds, own_ref, *refs):
    outs = refs[-len(kinds) :]
    hs, cs = refs[:8], refs[8:16]
    if 2 not in kinds:
        lhs, lo, hi, rows = refs[8:10], part * 2 + kinds[0], part * 2 + kinds[-1] + 1, hs
        values = dot(jnp.concatenate([r[lo * SLICE : hi * SLICE] for r in lhs], axis=1), stack(rows))
        values = [values[k * SLICE : (k + 1) * SLICE] for k in range(len(kinds))]
    elif kinds == (2,):
        lhs, rows = refs[8:10], hs
        values = [dot(jnp.concatenate([r[part * SLICE : (part + 1) * SLICE] for r in lhs], axis=1), stack(rows))]
    else:
        lo = part * 2 * SLICE
        lhs = [r[lo : lo + 2 * SLICE] for r in refs[16:18]]
        values = dot(jnp.concatenate(lhs, axis=1), stack(hs))
        values = [values[:SLICE], values[SLICE:]]
        lhs = [r[part * SLICE : (part + 1) * SLICE] for r in refs[18:20]]
        values.append(dot(jnp.concatenate(lhs, axis=1), stack(cs)))
    for out, value in zip(outs, values):
        if part == 0:
            out[0] = value.astype(BF16)
        else:
            out[...] = value.astype(BF16)


def expert_weights(part, kinds, own, hs, cs, dgu_t, act_t, after):
    wide = W_STEP
    hs, dgu_t = (hs, dgu_t) if 0 in kinds or 1 in kinds else ([], ())
    cs, act_t = (cs, act_t) if 2 in kinds else ([], ())
    specs, arrays = pieces(hs, cs, wide)
    if part == 0:
        made = pl.BlockSpec((1, SLICE, wide), lambda j, own: (own[0], 0, j))
        grad = jax.ShapeDtypeStruct((2, SLICE, D), BF16)
    else:
        made = pl.BlockSpec((SLICE, wide), lambda j, own: (0, j))
        grad = jax.ShapeDtypeStruct((SLICE, D), BF16)
    out = pl.pallas_call(
        functools.partial(weights_kernel, part, kinds),
        grid_spec=pltpu.PrefetchScalarGridSpec(
            num_scalar_prefetch=1,
            grid=(D // wide,),
            in_specs=specs
            + [whole((4 * SLICE, PART))] * len(dgu_t)
            + [whole((2 * SLICE, PART))] * len(act_t)
            + [pl.BlockSpec(memory_space=pl.ANY)] * len(after),
            out_specs=[made] * len(kinds),
        ),
        out_shape=[grad] * len(kinds),
        compiler_params=params(),
        cost_estimate=pl.CostEstimate(
            flops=2 * 2 * PART * len(kinds) * SLICE * D, bytes_accessed=len(kinds) * 6 << 20, transcendentals=0
        ),
        name="expert_weights",
    )(own, *arrays, *dgu_t, *act_t, *after)
    return list(out)


def pack_matrix():
    out = np.zeros((4 * ROWS, 4 * ROWS), np.float32)
    for quarter in range(4):
        for src in range(N_DP):
            for k in range(CAP):
                out[src * 4 * CAP + quarter * CAP + k, quarter * ROWS + src * CAP + k] = 1.0
    return out


def pack_kernel(m_ref, *refs):
    left, right, out_ref = refs[:3], refs[3:6], refs[6]

    def total(refs, cols):
        p, q, r = [x[:, cols].astype(F32) for x in refs]
        return p + q + r

    wide = 512
    for j in range(QUART // wide):
        lo = j * wide
        rows = [total(x, slice(at, at + wide)).astype(BF16) for x in (left, right) for at in (lo, lo + QUART)]
        out_ref[:, lo : lo + wide] = dot(m_ref[...], jnp.concatenate(rows, axis=0)).astype(BF16)
    pw = total(right, slice(HALF, HALF + EXTRA))
    pw = pw[:, 0:1] + pw[:, 1:2]
    high = pw.astype(BF16).astype(F32)
    lane = iota((ROWS, EXTRA), 1)
    value = jnp.where(lane == 0, high, jnp.where(lane == 1, pw - high, 0.0)).astype(BF16)
    out_ref[:, QUART:] = dot(m_ref[:, :ROWS], value).astype(BF16)


def pack(left, right):
    return pl.pallas_call(
        pack_kernel,
        out_shape=jax.ShapeDtypeStruct((4 * ROWS, QUART + EXTRA), BF16),
        compiler_params=params(),
        cost_estimate=pl.CostEstimate(flops=2 * 384 * 384 * QUART, bytes_accessed=4 << 20, transcendentals=0),
        name="pack_rows",
    )(jnp.asarray(pack_matrix(), BF16), *left, *right)


def combine_kernel(own_ref, r0_ref, r1_ref, h_ref, c_ref, gain_ref, rrow_ref, wrow_ref, out_ref, routes_ref):
    rank = rank_of(rrow_ref[...], 1)
    dp, when = place_of(column(rrow_ref[...]), own_ref)
    place = dp * (4 * CAP) + rank + when * (4 * ROWS)
    at = iota((TOK, 8 * ROWS), 1)
    r = jnp.concatenate([r0_ref[...], r1_ref[...]], axis=0)
    picks = [jnp.where(at == place + q * CAP, 1.0, 0.0).astype(BF16) for q in range(4)]
    pw = dot(picks[0], r[:, QUART:])
    diagonal = iota((TOK, TOK), 0) == iota((TOK, TOK), 1)
    pw = jnp.sum(jnp.where(diagonal, pw[:, 0:1] + pw[:, 1:2], 0.0), axis=0, keepdims=True)
    routes_ref[...] = pw / wrow_ref[...].astype(F32)
    g = jnp.concatenate([dot(p, r[:, :QUART]) for p in picks], axis=1)
    x = h_ref[...].astype(F32)
    scale = lax.rsqrt(jnp.mean(x * x, axis=-1, keepdims=True) + EPS)
    x = x * scale
    dx = g * gain_ref[...]
    mix = jnp.mean(dx * x, axis=-1, keepdims=True)
    out_ref[...] = (c_ref[...].astype(F32) + scale * (dx - x * mix)).astype(BF16)


def combine(own, r0, r1, h, c, gain, rrow, wrow):
    return pl.pallas_call(
        combine_kernel,
        in_specs=[pl.BlockSpec(memory_space=pltpu.SMEM)] + [pl.BlockSpec(memory_space=pltpu.VMEM)] * 7,
        out_shape=[
            jax.ShapeDtypeStruct((TOK, D), BF16),
            jax.ShapeDtypeStruct((1, TOK), F32),
        ],
        compiler_params=params(),
        cost_estimate=pl.CostEstimate(flops=2 * 128 * 768 * D, bytes_accessed=5 << 20, transcendentals=0),
        name="combine",
    )(own, r0, r1, h, c, gain, rrow, wrow)


def exchange(x):
    shaped = x.reshape((N_DP, -1) + x.shape[1:])
    got = lax.all_to_all(shaped, "dp", split_axis=0, concat_axis=0, tiled=True)
    return got.reshape(x.shape)


def body(h, c, gain, routes, w, w_gate, w_up, w_down):
    gain = gain.reshape(1, D)
    rrow, wrow = routes.reshape(1, TOK), w.reshape(1, TOK)
    own0, own1 = owned()
    owns = jnp.stack([own0, own1])
    mine = jnp.where((lax.axis_index("dp") & 1) == 0, own0, own1)
    own = mine.reshape(1)
    weights = (w_gate, w_up, w_down)

    slots_a = dispatch(1, owns, h, c, gain, rrow, wrow)
    (slots_b,) = dispatch(0, owns, tie(h, *slots_a), c, gain, rrow, wrow)
    slots_a = [trade_for(core, x).reshape(N_DP // 2, -1, HALF) for core, x in enumerate(slots_a)]
    got_b = exchange(slots_b)
    leave = [lax.dynamic_index_in_dim(x, 1 - mine, 0, keepdims=False) for x in weights]
    got_g = trade(leave[0])
    got_b, got_g, *slots_a, leave_u, leave_d = barrier(got_b, got_g, *slots_a, *leave[1:])
    got_u = trade(leave_u)
    bh, bc = sort_rows(got_b, 2)
    got_a = exchange(jnp.stack(slots_a, axis=1).reshape(4 * ROWS, HALF))
    got_a, got_u, bh, bc = barrier(got_a, got_u, bh, bc)
    got_d = trade(leave_d)
    (a,) = sort_rows(got_a, 1)
    az, ay = over_z(a), over_y(a)
    az, ay, bh, bc, got_d = barrier(az, ay, bh, bc, got_d)
    got = got_g, got_u, got_d
    ao, bzh, bzc, byh, byc = over_y(az), over_z(bh), over_z(bc), over_y(bh), over_y(bc)
    piece_a = (a, ay, az, ao)
    hs_a, cs_a = [(x, 0) for x in piece_a], [(x, 1) for x in piece_a]
    dgu_a, dgu_ta, act_ta, pw_a = forward(own, hs_a, cs_a, weights, got)
    bzh, bzc, byh, byc, dgu_a = barrier(bzh, bzc, byh, byc, dgu_a)
    boh, boc = over_y(bzh), over_y(bzc)
    la, ra, norm_a = expert_rows(own, dgu_a, pw_a, hs_a, weights, got)
    al, ar = reduce_first(la, ra)

    hs_b, cs_b = [(x, 0) for x in (bh, byh, bzh, boh)], [(x, 0) for x in (bc, byc, bzc, boc)]
    dgu_b, dgu_tb, act_tb, pw_b = forward(own, hs_b, cs_b, weights, got)
    dgu_b, *al, = barrier(dgu_b, *al)
    dgu_b, *ar, = barrier(dgu_b, *ar)
    al, ar = reduce_second(la, ra, al, ar)
    lb, rb, norm_b = expert_rows(own, dgu_b, pw_b, hs_b, weights, got)
    norm = (norm_a + norm_b) / gain
    hs, cs, dgu_t, act_t = hs_a + hs_b, cs_a + cs_b, (dgu_ta, dgu_tb), (act_ta, act_tb)
    grads = functools.partial(expert_weights, own=own, hs=hs, cs=cs, dgu_t=dgu_t, act_t=act_t)
    lb, rb, al, ar, norm = tree_barrier((lb, rb, al, ar, norm))
    bl, br = reduce_first(lb, rb)
    packed_a = pack(al, ar)
    norm, sent_a = barrier(sum_dp(norm, 1), packed_a)
    packed_a = trade(packed_a)
    (give_g,) = grads(1, (0,), after=(lb[0], sent_a, norm))
    norm, give_g = barrier(sum_dp(norm, 4), give_g)
    take_g = trade(give_g)
    (give_u,) = grads(1, (1,), after=(give_g, norm))
    norm, packed_a, give_u, *far = barrier(sum_dp(norm, 8), packed_a, give_u, *bl, *br)
    sum_l, sum_r = add(lb[1], far[0]), add(rb[2], far[2])
    sum_l, sum_r, packed_a, norm, give_u = barrier(sum_l, sum_r, packed_a, norm, give_u)
    bl, br = (lb[0], far[1], over_y(sum_l)), (rb[0], far[3], over_z(sum_r))
    take_u = trade(give_u)
    r_a = exchange(packed_a)
    mine_gud = grads(0, (0, 1, 2), after=(sum_l, sum_r))
    norm, mine_gud[0] = barrier(spread(sum_dp(norm, 2)), mine_gud[0])
    (give_d,) = grads(1, (2,), after=(mine_gud[0], norm))
    norm, give_d = barrier(norm + over_z(norm), give_d)
    norm = norm + over_y(norm)
    norm, *far = barrier(norm, *bl, *br)
    norm = norm + trade(norm)
    packed_b, r_a, take_g = barrier(pack(far[:3], far[3:]), r_a, take_g)
    r_b = exchange(packed_b)
    take_d = trade(give_d)
    r_b, take_u = barrier(r_b, take_u)
    norm = jnp.sum(norm, axis=0)
    grads = [
        lax.dynamic_update_index_in_dim(x, t, 1 - mine, 0)
        for x, t in zip(mine_gud, (take_g, take_u, take_d))
    ]
    r_b, *grads = barrier(r_b, *grads)
    out, grad_routes = combine(owns, r_b, r_a, h, c, gain, rrow, wrow)
    grad_routes = grad_routes.reshape(TOK, 1)
    return out, norm, grad_routes, *grads


def solution(mesh):
    tokens = P(("dp", "tensor"), None)
    weights = P("dp", "tensor", None)
    return jax.shard_map(
        body,
        mesh=mesh,
        in_specs=(tokens, tokens, P(), tokens, tokens, weights, weights, weights),
        out_specs=(tokens, P(), tokens, weights, weights, weights),
        check_vma=False,
    )
```
